32 devices in a mesh: groups: 2 (over y), pair: 4 (over z), mp: 2 (over x), side: 2 (over core).
Axes of the slice: x: 2, y: 2, z: 4, core: 2. Of those that a mesh axis runs over, the one named last changes fastest.
Arguments:
- past_frames: bfloat16 [32, 196, 1024], P(('groups', 'pair', 'side')), parts along dimension 0, may hold values from -6 to 6
- future_frames: bfloat16 [32, 196, 1024], P(('groups', 'pair', 'side')), parts along dimension 0, may hold values from -6 to 6
- visible: int32 [32, 196], P(('groups', 'pair', 'side')), parts along dimension 0, may hold values from 0 to 1, as said below
- partner: int32 [16, 2], P(('groups', 'pair', 'side')), parts along dimension 0, may hold values from 0 to 1, each once within a row
- enc_weight: bfloat16 [3, 1024, 1024], P(None, None, 'mp'), may hold values from -2 to 2
- embed_weight: bfloat16 [1024, 512], P('mp'), may hold values from -0.1875 to 0.1875
- mask_token: bfloat16 [512], replicated, may hold values from -4 to 4
- dec_pos: bfloat16 [196, 512], replicated, may hold values from -4 to 4
- dec_qkv: bfloat16 [3, 512, 512], P(None, None, 'mp'), may hold values from -0.25 to 0.25
- dec_out: bfloat16 [512, 512], P('mp'), may hold values from -0.25 to 0.25
- out_grad: bfloat16 [32, 196, 512], P(('groups', 'pair', 'side')), parts along dimension 0, may hold values from -6 to 6
Outputs:
- prediction: bfloat16 [32, 196, 512], P(('groups', 'pair', 'side')), parts along dimension 0
- enc_grad: float32 [6, 1024, 1024], P('groups', ('pair', 'side'), 'mp'), parts along dimension 0
- embed_grad: float32 [2048, 512], P(('groups', 'mp')), parts along dimension 0
- qkv_grad: float32 [6, 512, 512], P('groups', None, 'mp'), parts along dimension 0
- out_w_grad: float32 [1024, 512], P(('groups', 'mp')), parts along dimension 0
The draws below stay inside these ranges and needn't reach their ends.
There are 2 independent parts, one for each index of `groups`. The reference program is written for one: setup_inputs(seed, part) draws one part's arguments, and reference() takes and returns one part's arrays. A program takes and returns all parts, laid end to end along the dimension named above; an argument that names none is the same for every part. Nothing has to cross between parts.
Inputs may be any that keep to these rules, and one draw needn't show every extreme that they name: `visible`: every row holds exactly 10 ones. `partner`: each row is a permutation of 0 to 1.
All inputs are finite; a program needn't handle non-finite values.
Results may differ from the reference program's by a relative error of at most 0.033.
Values may be sent and summed in bfloat16 or wider, within the bound.
A program may use at most 128 MiB of HBM per device.

```python
import math
import jax
import jax.numpy as jnp
from jax import lax

D = 1024
DD = 512
NP = 196
VIS = 10
FR = 2
HD = 64
DHD = 32
HOLDERS = 8
PAIRS = 16
N_MP = 2


def draw_visible(key, part):
    key = jax.random.fold_in(key, 5)
    scores = jax.random.randint(key, (PAIRS, NP), 0, 1048576) * NP + jnp.arange(NP, dtype=jnp.int32)[None, :]
    ranks = jnp.argsort(jnp.argsort(scores, axis=1), axis=1)
    return (ranks < VIS).astype(jnp.int32)


def draw_enc_weight(key, part):
    key = jax.random.fold_in(key, 11)
    base = jax.random.normal(key, (3, D, D), jnp.float32) * D ** (-0.5)
    return jnp.clip(base, -2.0, 2.0).astype(jnp.bfloat16)


def block_levels(stream_key, shape, split, least, largest):
    loudness, own = 1.0, jax.random.fold_in(stream_key, 6)
    for dim, shards_of in split:
        heights = jnp.exp(jax.random.uniform(jax.random.fold_in(own, dim), (shards_of,), jnp.float32, least / len(split), largest / len(split)))
        loudness = loudness * jnp.repeat(heights, shape[dim] // shards_of).reshape([-1 if axis == dim else 1 for axis in range(len(shape))])
    return loudness


def gaussian(key, extent, scale, limit, pieces=(), held_as=jnp.bfloat16):
    entries = scale * jax.random.normal(key, extent, jnp.float32)
    if pieces:
        entries = entries * block_levels(key, extent, pieces, -0.22, 0.18)
    return jnp.clip(entries, -limit, limit).astype(held_as)


def setup_inputs(seed: int = 0, part: int = 0) -> dict:
    seeds = jax.random.split(jax.random.key(seed), 12)
    part_keys = jax.random.split(jax.random.fold_in(seeds[11], part), 12)
    return {
        "past_frames": gaussian(part_keys[0], (PAIRS, NP, D), 1.0, 6.0, ((0, 8),)),
        "future_frames": gaussian(part_keys[1], (PAIRS, NP, D), 1.0, 6.0, ((0, 8),)),
        "visible": draw_visible(jax.random.fold_in(jax.random.fold_in(seeds[11], part), 71), part),
        "partner": jax.vmap(lambda own: jax.random.permutation(own, FR))(jax.random.split(part_keys[3], HOLDERS)).reshape((HOLDERS, FR)).astype(jnp.int32),
        "enc_weight": draw_enc_weight(jax.random.fold_in(seeds[11], 71), part),
        "embed_weight": gaussian(seeds[5], (D, DD), D ** -0.5, 0.1875, ((0, 2),)),
        "mask_token": gaussian(seeds[6], (DD,), 1.0, 4.0),
        "dec_pos": gaussian(seeds[7], (NP, DD), 0.7, 4.0),
        "dec_qkv": gaussian(seeds[8], (3, DD, DD), DD ** -0.5, 0.25, ((2, 2),)),
        "dec_out": gaussian(seeds[9], (DD, DD), DD ** -0.5, 0.25, ((0, 2),)),
        "out_grad": gaussian(part_keys[10], (PAIRS, NP, DD), 1.0, 6.0, ((0, 8),)),
    }


EPS = 1e-06

def normalize(tokens):
    wide = tokens.astype(jnp.float32)
    centred = wide - lax.optimization_barrier(jnp.mean(wide, axis=-1, keepdims=True))
    return centred * lax.rsqrt(lax.optimization_barrier(jnp.mean(centred * centred, axis=-1, keepdims=True)) + EPS)

def normalize_back(tokens, cotangent):
    wide = tokens.astype(jnp.float32)
    centred = wide - lax.optimization_barrier(jnp.mean(wide, axis=-1, keepdims=True))
    inverse = lax.rsqrt(lax.optimization_barrier(jnp.mean(centred * centred, axis=-1, keepdims=True)) + EPS)
    unit = centred * inverse
    return inverse * (cotangent - lax.optimization_barrier(jnp.mean(cotangent, axis=-1, keepdims=True)) - unit * lax.optimization_barrier(jnp.mean(cotangent * unit, axis=-1, keepdims=True)))

def frame_heads(tokens, head_size):
    return tokens.astype(jnp.float32).reshape(tokens.shape[0], -1, head_size)

def frame_probs(query, keys, head_size):
    scores = jnp.einsum('rhd,shd->hrs', frame_heads(query, head_size), frame_heads(keys, head_size)) / math.sqrt(head_size)
    return jax.nn.softmax(scores, axis=-1)

def frame_attend(query, keys, values, head_size):
    probs = frame_probs(query, keys, head_size)
    weights = lax.optimization_barrier(probs.astype(jnp.bfloat16)).astype(jnp.float32)
    mixed = jnp.einsum('hrs,shd->rhd', weights, frame_heads(values, head_size))
    return mixed.reshape(query.shape).astype(jnp.bfloat16)

def frame_attend_back(query, keys, values, upstream, head_size):
    probs = frame_probs(query, keys, head_size)
    weights = lax.optimization_barrier(probs.astype(jnp.bfloat16)).astype(jnp.float32)
    grad_heads = frame_heads(upstream, head_size)
    grad_probs = jnp.einsum('rhd,shd->hrs', grad_heads, frame_heads(values, head_size))
    grad_values = jnp.einsum('hrs,rhd->shd', weights, grad_heads).reshape(values.shape).astype(jnp.bfloat16)
    grad_scores = probs * (grad_probs - lax.optimization_barrier(jnp.sum(grad_probs * probs, axis=-1, keepdims=True))) / math.sqrt(head_size)
    grad_scores = lax.optimization_barrier(grad_scores.astype(jnp.bfloat16)).astype(jnp.float32)
    grad_query = jnp.einsum('hrs,shd->rhd', grad_scores, frame_heads(keys, head_size)).reshape(query.shape).astype(jnp.bfloat16)
    grad_keys = jnp.einsum('hrs,rhd->shd', grad_scores, frame_heads(query, head_size)).reshape(keys.shape).astype(jnp.bfloat16)
    return (grad_query, grad_keys, grad_values)

def split_sum(factor_pairs):
    total = None
    for member in range(N_MP):
        term = None
        for first_arr, second_arr in factor_pairs:
            span_size = second_arr.shape[0] // N_MP
            piece = jnp.dot(first_arr[:, member * span_size:(member + 1) * span_size], second_arr[member * span_size:(member + 1) * span_size], preferred_element_type=jnp.float32)
            term = piece if term is None else term + piece
        term = lax.optimization_barrier(term.astype(jnp.bfloat16)).astype(jnp.float32)
        total = term if total is None else total + term
    return total

def attend_all(query, keys, values, head_size):
    return lax.map(lambda items: frame_attend(items[0], items[1], items[2], head_size), (query, keys, values))

def attend_back_all(query, keys, values, upstream, head_size):
    return lax.map(lambda items: frame_attend_back(items[0], items[1], items[2], items[3], head_size), (query, keys, values, upstream))

def reference(past_frames, future_frames, visible, partner, enc_weight, embed_weight, mask_token, dec_pos, dec_qkv, dec_out, out_grad):
    past_count = PAIRS * NP
    slots = jnp.cumsum(visible, axis=1) - 1
    select = ((visible[:, None, :] == 1) & (slots[:, None, :] == jnp.arange(VIS)[None, :, None])).astype(jnp.float32)
    seen = jnp.einsum('fjn,fnd->fjd', select, future_frames.astype(jnp.float32)).astype(jnp.bfloat16)
    every_row = jnp.concatenate([past_frames.reshape(-1, D), seen.reshape(-1, D)], axis=0)
    normed_rows = normalize(every_row).astype(jnp.bfloat16)
    projected = [jnp.dot(normed_rows, enc_weight[index], preferred_element_type=jnp.float32).astype(jnp.bfloat16) for index in range(3)]
    past_split = tuple((item[:past_count].reshape(PAIRS, NP, D) for item in projected))
    seen_split = tuple((item[past_count:].reshape(PAIRS, VIS, D) for item in projected))
    past_att = attend_all(past_split[0], past_split[1], past_split[2], HD)
    seen_att = attend_all(seen_split[0], seen_split[1], seen_split[2], HD)
    att_rows = jnp.concatenate([past_att.reshape(-1, D), seen_att.reshape(-1, D)], axis=0)
    embedded = split_sum([(att_rows, embed_weight)]).astype(jnp.bfloat16)
    past_emb = embedded[:past_count].reshape(PAIRS, NP, DD)
    seen_emb = embedded[past_count:].reshape(PAIRS, VIS, DD)
    key_source = (past_emb.astype(jnp.float32) + dec_pos.astype(jnp.float32)).astype(jnp.bfloat16)
    holder = jnp.arange(PAIRS, dtype=jnp.int32) // FR
    source = ((holder + HOLDERS // 2) % HOLDERS * FR + partner.reshape(-1)).astype(jnp.int32)
    paired = key_source[source]
    placed = jnp.einsum('fjn,fjd->fnd', select, seen_emb.astype(jnp.float32))
    hidden_mask = 1.0 - visible.astype(jnp.float32)
    decoder_in = (placed + hidden_mask[:, :, None] * mask_token.astype(jnp.float32) + dec_pos.astype(jnp.float32)).astype(jnp.bfloat16)
    normed_dec = normalize(decoder_in).astype(jnp.bfloat16)
    dec_query = jnp.dot(normed_dec.reshape(-1, DD), dec_qkv[0], preferred_element_type=jnp.float32).astype(jnp.bfloat16).reshape(PAIRS, NP, DD)
    dec_keys = jnp.dot(paired.reshape(-1, DD), dec_qkv[1], preferred_element_type=jnp.float32).astype(jnp.bfloat16).reshape(PAIRS, NP, DD)
    dec_values = jnp.dot(paired.reshape(-1, DD), dec_qkv[2], preferred_element_type=jnp.float32).astype(jnp.bfloat16).reshape(PAIRS, NP, DD)
    context = attend_all(dec_query, dec_keys, dec_values, DHD)
    update = split_sum([(context.reshape(-1, DD), dec_out)])
    prediction = (decoder_in.reshape(-1, DD).astype(jnp.float32) + update).astype(jnp.bfloat16).reshape(PAIRS, NP, DD)
    upstream = out_grad.reshape(-1, DD)
    out_w_grad = jnp.dot(context.reshape(-1, DD).T, upstream, preferred_element_type=jnp.float32)
    context_grad = jnp.dot(upstream, dec_out.T, preferred_element_type=jnp.float32).astype(jnp.bfloat16).reshape(PAIRS, NP, DD)
    query_grad, keys_grad, values_grad = attend_back_all(dec_query, dec_keys, dec_values, context_grad, DHD)
    qkv_grad = jnp.stack([jnp.dot(normed_dec.reshape(-1, DD).T, query_grad.reshape(-1, DD), preferred_element_type=jnp.float32), jnp.dot(paired.reshape(-1, DD).T, keys_grad.reshape(-1, DD), preferred_element_type=jnp.float32), jnp.dot(paired.reshape(-1, DD).T, values_grad.reshape(-1, DD), preferred_element_type=jnp.float32)])
    normed_grad = split_sum([(query_grad.reshape(-1, DD), dec_qkv[0].T)])
    pair_grad = split_sum([(keys_grad.reshape(-1, DD), dec_qkv[1].T), (values_grad.reshape(-1, DD), dec_qkv[2].T)])
    input_grad = out_grad.reshape(-1, DD).astype(jnp.float32) + normalize_back(decoder_in.reshape(-1, DD), normed_grad)
    seen_emb_grad = jnp.einsum('fjn,fnd->fjd', select, input_grad.reshape(PAIRS, NP, DD), precision=lax.Precision.HIGHEST).astype(jnp.bfloat16)
    past_emb_grad = jnp.zeros((PAIRS, NP, DD), jnp.float32).at[source].set(pair_grad.reshape(PAIRS, NP, DD)).astype(jnp.bfloat16)
    emb_rows_grad = jnp.concatenate([past_emb_grad.reshape(-1, DD), seen_emb_grad.reshape(-1, DD)], axis=0)
    embed_grad = jnp.dot(att_rows.T, emb_rows_grad, preferred_element_type=jnp.float32)
    att_grad = jnp.dot(emb_rows_grad, embed_weight.T, preferred_element_type=jnp.float32).astype(jnp.bfloat16)
    past_grads = attend_back_all(past_split[0], past_split[1], past_split[2], att_grad[:past_count].reshape(PAIRS, NP, D), HD)
    seen_grads = attend_back_all(seen_split[0], seen_split[1], seen_split[2], att_grad[past_count:].reshape(PAIRS, VIS, D), HD)
    enc_grad = jnp.stack([jnp.dot(normed_rows.T, jnp.concatenate([past_grads[index].reshape(-1, D), seen_grads[index].reshape(-1, D)], axis=0), preferred_element_type=jnp.float32) for index in range(3)])
    return (prediction, enc_grad, embed_grad, qkv_grad, out_w_grad)
```

```python
import functools
import math

import jax
import jax.numpy as jnp
from jax import lax
from jax.experimental import pallas as pl
from jax.experimental.pallas import tpu as pltpu
from jax.sharding import PartitionSpec as P

VIS = 10
VP = 16
HD = 64
DHD = 32
EPS = 1e-06
F32 = jnp.float32
BF16 = jnp.bfloat16
VMEM_LIMIT = 56 * 1024 * 1024


def dot(a, b):
    return jnp.dot(a, b, preferred_element_type=F32)


def dot_t(a, b):
    return lax.dot_general(a, b, (((1,), (1,)), ((), ())), preferred_element_type=F32)


def flip(a):
    return a.astype(F32).T


def normalize(wide):
    centred = wide - jnp.mean(wide, axis=-1, keepdims=True)
    return centred * lax.rsqrt(jnp.mean(centred * centred, axis=-1, keepdims=True) + EPS)


def softmax(scores):
    e = jnp.exp(scores - jnp.max(scores, axis=-1, keepdims=True))
    return e * (1.0 / jnp.sum(e, axis=-1, keepdims=True))


def head_cols(h, hs, x):
    lane = lax.broadcasted_iota(jnp.int32, x.shape, 1)
    return jnp.where((lane >= h * hs) & (lane < (h + 1) * hs), x, jnp.zeros_like(x))


def attention(q, k, v, hs, up=None, forward=True, mask=None):
    scale = 1.0 / math.sqrt(hs)
    ctx = dq = None
    dkt, dvt = [], []
    if up is not None:
        upt = flip(up).astype(BF16)
        qt = flip(q).astype(BF16)
    for h in range(q.shape[1] // hs):
        s = dot_t(head_cols(h, hs, q), k) * scale
        if mask is not None:
            s = jnp.where(mask, s, -1e30)
        p = softmax(s)
        w = p.astype(BF16)
        if forward:
            c = dot(w, head_cols(h, hs, v))
            ctx = c if ctx is None else ctx + c
        if up is not None:
            dp = dot_t(head_cols(h, hs, up), v)
            dvt.append(dot(upt[h * hs : (h + 1) * hs], w))
            ds = (p * (dp - jnp.sum(dp * p, axis=-1, keepdims=True)) * scale).astype(BF16)
            d = dot(ds, head_cols(h, hs, k))
            dq = d if dq is None else dq + d
            dkt.append(dot(qt[h * hs : (h + 1) * hs], ds))
    out = []
    if forward:
        out.append(ctx.astype(BF16))
    if up is not None:
        out += [
            dq.astype(BF16),
            jnp.concatenate(dkt, 0).T.astype(BF16),
            jnp.concatenate(dvt, 0).T.astype(BF16),
        ]
    return out


def groups_of(ref):
    n = ref.shape[-1]
    return [slice(i, i + 128) for i in range(0, n, 128)]


def select_of(visible):
    n = visible.shape[1]
    lower = lax.broadcasted_iota(jnp.int32, (n, n), 0) <= lax.broadcasted_iota(jnp.int32, (n, n), 1)
    rank = dot(visible.astype(F32).astype(BF16), lower.astype(F32).astype(BF16))
    row = lax.broadcasted_iota(jnp.int32, (VP, n), 0).astype(F32) + 1.0
    picks = (row == rank) & (visible.astype(F32) > 0.5)
    return picks.astype(F32).astype(BF16)


def total(refs, index=None):
    acc = None
    for r in refs:
        x = (r[...] if index is None else r[index]).astype(F32)
        acc = x if acc is None else acc + x
    return acc


def seen_mask(rows):
    a = lax.broadcasted_iota(jnp.int32, (rows, rows), 0)
    b = lax.broadcasted_iota(jnp.int32, (rows, rows), 1)
    return (a // VP == b // VP) & (b % VP < VIS)


def seen_kernel(fut, vis, wenc, wemb, normed, proj, att, part):
    for j in range(fut.shape[0]):
        sel = select_of(vis[j : j + 1, :])
        seen = dot(sel, fut[j]).astype(BF16)
        normed[j * VP : (j + 1) * VP, :] = normalize(seen.astype(F32)).astype(BF16)
    x = normed[...]
    for c in range(3):
        proj[c] = dot(x, wenc[c]).astype(BF16)
    mask = seen_mask(x.shape[0])
    for g in groups_of(att):
        (att[:, g],) = attention(proj[0, :, g], proj[1, :, g], proj[2, :, g], HD, mask=mask)
    part[...] = dot(att[...], wemb[...]).astype(BF16)


def query_kernel(n_mp, vis, mask_token, pos, wq, wout, og, *refs):
    parts = refs[:n_mp]
    dec_in, normed, query, cgrad = refs[n_mp:]
    for j in range(og.shape[0]):
        v = vis[j : j + 1, :]
        sel = select_of(v)
        emb = total(parts, (slice(j * VP, (j + 1) * VP), slice(None))).astype(BF16)
        placed = dot(flip(sel).astype(BF16), emb)
        hidden = 1.0 - flip(jnp.broadcast_to(v, (8, v.shape[1])))[:, :1]
        d = (placed + hidden * mask_token[...].astype(F32) + pos[...].astype(F32)).astype(BF16)
        dec_in[j] = d
        x = normalize(d.astype(F32)).astype(BF16)
        normed[j] = x
        query[j] = dot(x, wq[0]).astype(BF16)
        cgrad[j] = dot_t(og[j], wout[...]).astype(BF16)


def encode_kernel(j, flags, own, other, wenc, wemb, normed, proj, att, part):
    x = jnp.where(flags[j] == 1, own[...].astype(F32), other[...].astype(F32))
    normed[...] = normalize(x).astype(BF16)
    for c in range(3):
        proj[c] = dot(normed[...], wenc[c]).astype(BF16)
    for g in groups_of(att):
        (att[:, g],) = attention(proj[0, :, g], proj[1, :, g], proj[2, :, g], HD)
    part[...] = dot(att[...], wemb[...]).astype(BF16)


def decode_kernel(j, n_mp, vis, pos, wqkv, wout, query, cgrad, *refs):
    parts = refs[:n_mp]
    paired, ctx, dq, dk, dv, update, pair_part, vis_part, keys, values = refs[n_mp:]
    emb = total(parts).astype(BF16)
    paired[...] = (emb.astype(F32) + pos[...].astype(F32)).astype(BF16)
    keys[...] = dot(paired[...], wqkv[1]).astype(BF16)
    values[...] = dot(paired[...], wqkv[2]).astype(BF16)
    for g in groups_of(ctx):
        ctx[:, g], dq[:, g], dk[:, g], dv[:, g] = attention(
            query[j, :, g], keys[:, g], values[:, g], DHD, up=cgrad[j, :, g]
        )
    pair_part[...] = (dot_t(dk[...], wqkv[1]) + dot_t(dv[...], wqkv[2])).astype(BF16)
    chosen = dot(select_of(vis[j : j + 1, :]), dq[...]).astype(BF16)
    vis_part[...] = dot_t(chosen, wqkv[0]).astype(BF16)
    update[...] = dot(ctx[...], wout[...]).astype(BF16)


def decoder_weights_kernel(normed, og, p0, p1, c0, c1, q0, q1, k0, k1, v0, v1, qkv, wout):
    def term(a0, a1, b0, b1):
        return dot(flip(a0).astype(BF16), b0) + dot(flip(a1).astype(BF16), b1)

    qkv[0] = term(normed[0], normed[1], q0[...], q1[...]).astype(qkv.dtype)
    pt0, pt1 = flip(p0[...]).astype(BF16), flip(p1[...]).astype(BF16)
    qkv[1] = (dot(pt0, k0[...]) + dot(pt1, k1[...])).astype(qkv.dtype)
    qkv[2] = (dot(pt0, v0[...]) + dot(pt1, v1[...])).astype(qkv.dtype)
    wout[...] = term(c0[...], c1[...], og[0], og[1]).astype(wout.dtype)


def encode_back_kernel(n_mp, wemb, proj, *refs):
    parts = refs[:n_mp]
    grad, dproj, att_grad = refs[n_mp:]
    grad[...] = total(parts).astype(BF16)
    att_grad[...] = dot_t(grad[...], wemb[...]).astype(BF16)
    for g in groups_of(att_grad):
        dproj[0, :, g], dproj[1, :, g], dproj[2, :, g] = attention(
            proj[0, :, g], proj[1, :, g], proj[2, :, g], HD, up=att_grad[:, g], forward=False
        )


def seen_back_kernel(n_mp, vis, og, dec_in, wemb, proj, *refs):
    parts = (refs[:n_mp], refs[n_mp : 2 * n_mp])
    grad, dproj, att_grad = refs[2 * n_mp :]
    for j in range(2):
        sel = select_of(vis[j : j + 1, :])
        cot = total(parts[j])
        wide = dot(sel, dec_in[j])
        out = dot(sel, og[j])
        centred = wide - jnp.mean(wide, axis=-1, keepdims=True)
        inverse = lax.rsqrt(jnp.mean(centred * centred, axis=-1, keepdims=True) + EPS)
        unit = centred * inverse
        back = inverse * (
            cot
            - jnp.mean(cot, axis=-1, keepdims=True)
            - unit * jnp.mean(cot * unit, axis=-1, keepdims=True)
        )
        grad[j * VP : (j + 1) * VP, :] = (out + back).astype(BF16)
    att_grad[...] = dot_t(grad[...], wemb[...]).astype(BF16)
    mask = seen_mask(grad.shape[0])
    for g in groups_of(att_grad):
        dproj[0, :, g], dproj[1, :, g], dproj[2, :, g] = attention(
            proj[0, :, g], proj[1, :, g], proj[2, :, g], HD,
            up=att_grad[:, g], forward=False, mask=mask,
        )


def embed_weights_kernel(a0, a1, sa, g0, g1, sg, out):
    out[...] = (
        dot(flip(a0[...]).astype(BF16), g0[...])
        + dot(flip(a1[...]).astype(BF16), g1[...])
        + dot(flip(sa[...]).astype(BF16), sg[...])
    ).astype(out.dtype)


def encoder_weights_kernel(n0, n1, sn, d0, d1, sd, out):
    rows = 256
    for r in range(0, n0.shape[1], rows):
        cut = slice(r, r + rows)
        t0 = flip(n0[:, cut]).astype(BF16)
        t1 = flip(n1[:, cut]).astype(BF16)
        ts = flip(sn[:, cut]).astype(BF16)
        for c in range(3):
            out[c, cut, :] = (dot(t0, d0[c]) + dot(t1, d1[c]) + dot(ts, sd[c])).astype(out.dtype)


def call(kernel, outs, args, scratch=(), smem=0, flops=0):
    specs = [pl.BlockSpec(memory_space=pltpu.SMEM)] * smem
    specs += [pl.BlockSpec(memory_space=pltpu.VMEM)] * (len(args) - smem)
    bytes_moved = sum(a.size * a.dtype.itemsize for a in args) + sum(
        math.prod(s) * jnp.dtype(t).itemsize for s, t in outs
    )
    return pl.pallas_call(
        kernel,
        out_shape=[jax.ShapeDtypeStruct(s, t) for s, t in outs],
        in_specs=specs,
        out_specs=[pl.BlockSpec(memory_space=pltpu.VMEM)] * len(outs),
        scratch_shapes=[pltpu.VMEM(s, t) for s, t in scratch],
        compiler_params=pltpu.CompilerParams(vmem_limit_bytes=VMEM_LIMIT),
        cost_estimate=pl.CostEstimate(
            flops=flops, bytes_accessed=bytes_moved, transcendentals=0
        ),
    )(*args)


def shifted(x, axis, k):
    n = lax.axis_size(axis)
    return lax.ppermute(x, axis, [(i, (i + k) % n) for i in range(n)])


def all_parts(x):
    return [x] + [shifted(x, "mp", k) for k in range(1, lax.axis_size("mp"))]


def body(past, future, visible, partner, wenc, wemb, mask_token, pos, wqkv, wout, og):
    frames, np_, width = past.shape
    dd = pos.shape[1]
    n_mp = lax.axis_size("mp")
    half = lax.axis_size("pair") // 2
    ew, dw = wenc.shape[2], wqkv.shape[2]
    big = 6_000_000_000

    me = lax.axis_index("mp")
    if n_mp == frames:
        mine = shifted(lax.dynamic_index_in_dim(past, me, 0, keepdims=False), "pair", half)
        other = shifted(mine, "mp", 1)
        flags = (partner[0] == me).astype(jnp.int32)
    else:
        moved = shifted(past, "pair", half)
        mine, other = moved[0], moved[1]
        flags = (partner[0] == 0).astype(jnp.int32)

    sr = frames * VP
    seen_normed, seen_proj, seen_att, seen_part = call(
        seen_kernel,
        [((sr, width), BF16), ((3, sr, ew), BF16), ((sr, ew), BF16), ((sr, dd), BF16)],
        (future, visible, wenc, wemb), flops=big // 4,
    )
    dec_in, normed_dec, query, cgrad = call(
        functools.partial(query_kernel, n_mp),
        [((frames, np_, dd), BF16)] * 2 + [((frames, np_, dw), BF16)] * 2,
        (visible, mask_token.reshape(1, dd), pos, wqkv, wout, og, *all_parts(seen_part)),
        flops=big // 4,
    )
    enc = [
        call(
            functools.partial(encode_kernel, j),
            [((np_, width), BF16), ((3, np_, ew), BF16), ((np_, ew), BF16), ((np_, dd), BF16)],
            (flags, mine, other, wenc, wemb), smem=1, flops=big,
        )
        for j in range(frames)
    ]
    emb_parts = [all_parts(e[3]) for e in enc]
    dec = [
        call(
            functools.partial(decode_kernel, j, n_mp),
            [((np_, dd), BF16)] + [((np_, dw), BF16)] * 4
            + [((np_, dd), BF16)] * 2 + [((VP, dd), BF16)],
            (visible, pos, wqkv, wout, query, cgrad, *emb_parts[j]),
            scratch=[((np_, dw), BF16)] * 2, flops=big,
        )
        for j in range(frames)
    ]
    paired, ctx, dq, dk, dv, update, pair_part, vis_part = zip(*dec)
    pair_parts = [all_parts(x) for x in pair_part]
    vis_parts = [all_parts(x) for x in vis_part]
    updates = [all_parts(x) for x in update]
    qkv_term, out_term = call(
        decoder_weights_kernel,
        [(wqkv.shape, BF16), (wout.shape, BF16)],
        (normed_dec, og, *paired, *ctx, *dq, *dk, *dv), flops=big // 2,
    )
    seen_grad, seen_dproj = call(
        functools.partial(seen_back_kernel, n_mp),
        [((sr, dd), BF16), ((3, sr, ew), BF16)],
        (visible, og, dec_in, wemb, seen_proj, *vis_parts[0], *vis_parts[1]),
        scratch=[((sr, ew), BF16)], flops=big // 4,
    )
    back = [
        call(
            functools.partial(encode_back_kernel, n_mp),
            [((np_, dd), BF16), ((3, np_, ew), BF16)],
            (wemb, enc[j][1], *pair_parts[j]),
            scratch=[((np_, ew), BF16)], flops=big,
        )
        for j in range(frames)
    ]
    (embed_term,) = call(
        embed_weights_kernel, [(wemb.shape, BF16)],
        (enc[0][2], enc[1][2], seen_att, back[0][0], back[1][0], seen_grad), flops=big // 4,
    )
    (enc_term,) = call(
        encoder_weights_kernel, [(wenc.shape, BF16)],
        (enc[0][0], enc[1][0], seen_normed, back[0][1], back[1][1], seen_dproj), flops=big,
    )
    prediction = jnp.stack([
        (dec_in[j].astype(F32) + sum(u.astype(F32) for u in updates[j])).astype(BF16)
        for j in range(frames)
    ])
    enc_grad = lax.psum_scatter(
        enc_term, ("pair", "side"), scatter_dimension=1, tiled=True
    ).astype(F32)
    embed_grad, qkv_grad, out_grad = lax.psum(
        (embed_term, qkv_term, out_term), ("pair", "side")
    )
    return (
        prediction, enc_grad, embed_grad.astype(F32), qkv_grad.astype(F32), out_grad.astype(F32)
    )


def solution(mesh):
    rows = ("groups", "pair", "side")
    in_specs = (
        P(rows, None, None),
        P(rows, None, None),
        P(rows, None),
        P(rows, None),
        P(None, None, "mp"),
        P("mp", None),
        P(),
        P(),
        P(None, None, "mp"),
        P("mp", None),
        P(rows, None, None),
    )
    out_specs = (
        P(rows, None, None),
        P("groups", ("pair", "side"), "mp"),
        P(("groups", "mp"), None),
        P("groups", None, "mp"),
        P(("groups", "mp"), None),
    )
    return jax.shard_map(body, mesh=mesh, in_specs=in_specs, out_specs=out_specs, check_vma=False)
```

```python
import functools
import math

import jax
import jax.numpy as jnp
from jax import lax
from jax.experimental import pallas as pl
from jax.experimental.pallas import tpu as pltpu
from jax.sharding import PartitionSpec as P

VIS = 10
VP = 16
HD = 64
DHD = 32
EPS = 1e-06
F32 = jnp.float32
BF16 = jnp.bfloat16
VMEM_LIMIT = 56 * 1024 * 1024


def dot(a, b):
    return jnp.dot(a, b, preferred_element_type=F32)


def dot_t(a, b):
    return lax.dot_general(a, b, (((1,), (1,)), ((), ())), preferred_element_type=F32)


def flip(a):
    return a.astype(F32).T


def normalize(wide):
    centred = wide - jnp.mean(wide, axis=-1, keepdims=True)
    return centred * lax.rsqrt(jnp.mean(centred * centred, axis=-1, keepdims=True) + EPS)


def softmax(scores):
    e = jnp.exp(scores - jnp.max(scores, axis=-1, keepdims=True))
    return e * (1.0 / jnp.sum(e, axis=-1, keepdims=True))


def head_cols(h, hs, x):
    lane = lax.broadcasted_iota(jnp.int32, x.shape, 1)
    return jnp.where((lane >= h * hs) & (lane < (h + 1) * hs), x, jnp.zeros_like(x))


def attention(q, k, v, hs, up=None, forward=True, mask=None):
    scale = 1.0 / math.sqrt(hs)
    ctx = dq = None
    dkt, dvt = [], []
    if up is not None:
        upt = flip(up).astype(BF16)
        qt = flip(q).astype(BF16)
    for h in range(q.shape[1] // hs):
        s = dot_t(head_cols(h, hs, q), k) * scale
        if mask is not None:
            s = jnp.where(mask, s, -1e30)
        p = softmax(s)
        w = p.astype(BF16)
        if forward:
            c = dot(w, head_cols(h, hs, v))
            ctx = c if ctx is None else ctx + c
        if up is not None:
            dp = dot_t(head_cols(h, hs, up), v)
            dvt.append(dot(upt[h * hs : (h + 1) * hs], w))
            ds = (p * (dp - jnp.sum(dp * p, axis=-1, keepdims=True)) * scale).astype(BF16)
            d = dot(ds, head_cols(h, hs, k))
            dq = d if dq is None else dq + d
            dkt.append(dot(qt[h * hs : (h + 1) * hs], ds))
    out = []
    if forward:
        out.append(ctx.astype(BF16))
    if up is not None:
        out += [
            dq.astype(BF16),
            jnp.concatenate(dkt, 0).T.astype(BF16),
            jnp.concatenate(dvt, 0).T.astype(BF16),
        ]
    return out


def groups_of(ref):
    n = ref.shape[-1]
    return [slice(i, i + 128) for i in range(0, n, 128)]


def select_of(visible):
    n = visible.shape[1]
    lower = lax.broadcasted_iota(jnp.int32, (n, n), 0) <= lax.broadcasted_iota(jnp.int32, (n, n), 1)
    rank = dot(visible.astype(F32).astype(BF16), lower.astype(F32).astype(BF16))
    row = lax.broadcasted_iota(jnp.int32, (VP, n), 0).astype(F32) + 1.0
    picks = (row == rank) & (visible.astype(F32) > 0.5)
    return picks.astype(F32).astype(BF16)


def total(refs, index=None):
    acc = None
    for r in refs:
        x = (r[...] if index is None else r[index]).astype(F32)
        acc = x if acc is None else acc + x
    return acc


def seen_mask(rows):
    a = lax.broadcasted_iota(jnp.int32, (rows, rows), 0)
    b = lax.broadcasted_iota(jnp.int32, (rows, rows), 1)
    return (a // VP == b // VP) & (b % VP < VIS)


def seen_kernel(fut, vis, wenc, wemb, normed, proj, att, part):
    for j in range(fut.shape[0]):
        sel = select_of(vis[j : j + 1, :])
        seen = dot(sel, fut[j]).astype(BF16)
        normed[j * VP : (j + 1) * VP, :] = normalize(seen.astype(F32)).astype(BF16)
    x = normed[...]
    for c in range(3):
        proj[c] = dot(x, wenc[c]).astype(BF16)
    mask = seen_mask(x.shape[0])
    for g in groups_of(att):
        (att[:, g],) = attention(proj[0, :, g], proj[1, :, g], proj[2, :, g], HD, mask=mask)
    part[...] = dot(att[...], wemb[...]).astype(BF16)


def query_kernel(n_mp, vis, mask_token, pos, wq, wout, og, *refs):
    parts = refs[:n_mp]
    dec_in, normed, query, cgrad = refs[n_mp:]
    for j in range(og.shape[0]):
        v = vis[j : j + 1, :]
        sel = select_of(v)
        emb = total(parts, (slice(j * VP, (j + 1) * VP), slice(None))).astype(BF16)
        placed = dot(flip(sel).astype(BF16), emb)
        hidden = 1.0 - flip(jnp.broadcast_to(v, (8, v.shape[1])))[:, :1]
        d = (placed + hidden * mask_token[...].astype(F32) + pos[...].astype(F32)).astype(BF16)
        dec_in[j] = d
        x = normalize(d.astype(F32)).astype(BF16)
        normed[j] = x
        query[j] = dot(x, wq[0]).astype(BF16)
        cgrad[j] = dot_t(og[j], wout[...]).astype(BF16)


def encode_kernel(n_mp, where, *refs):
    parts = refs[:n_mp]
    wenc, wemb, normed, proj, att, part, whole = refs[n_mp:]
    span = parts[0].shape[1]
    for k in range(n_mp):
        whole[:, pl.ds(pl.multiple_of(where[k] * span, span), span)] = parts[k][...]
    normed[...] = normalize(whole[...].astype(F32)).astype(BF16)
    for c in range(3):
        proj[c] = dot(normed[...], wenc[c]).astype(BF16)
    for g in groups_of(att):
        (att[:, g],) = attention(proj[0, :, g], proj[1, :, g], proj[2, :, g], HD)
    part[...] = dot(att[...], wemb[...]).astype(BF16)


def decode_kernel(j, n_mp, vis, pos, wqkv, wout, query, cgrad, *refs):
    parts = refs[:n_mp]
    paired, ctx, dq, dk, dv, update, pair_part, vis_part, keys, values = refs[n_mp:]
    emb = total(parts).astype(BF16)
    paired[...] = (emb.astype(F32) + pos[...].astype(F32)).astype(BF16)
    keys[...] = dot(paired[...], wqkv[1]).astype(BF16)
    values[...] = dot(paired[...], wqkv[2]).astype(BF16)
    for g in groups_of(ctx):
        ctx[:, g], dq[:, g], dk[:, g], dv[:, g] = attention(
            query[j, :, g], keys[:, g], values[:, g], DHD, up=cgrad[j, :, g]
        )
    pair_part[...] = (dot_t(dk[...], wqkv[1]) + dot_t(dv[...], wqkv[2])).astype(BF16)
    chosen = dot(select_of(vis[j : j + 1, :]), dq[...]).astype(BF16)
    vis_part[...] = dot_t(chosen, wqkv[0]).astype(BF16)
    update[...] = dot(ctx[...], wout[...]).astype(BF16)


def decoder_weights_kernel(normed, og, p0, p1, c0, c1, q0, q1, k0, k1, v0, v1, qkv, wout):
    def term(a0, a1, b0, b1):
        return dot(flip(a0).astype(BF16), b0) + dot(flip(a1).astype(BF16), b1)

    qkv[0] = term(normed[0], normed[1], q0[...], q1[...]).astype(qkv.dtype)
    pt0, pt1 = flip(p0[...]).astype(BF16), flip(p1[...]).astype(BF16)
    qkv[1] = (dot(pt0, k0[...]) + dot(pt1, k1[...])).astype(qkv.dtype)
    qkv[2] = (dot(pt0, v0[...]) + dot(pt1, v1[...])).astype(qkv.dtype)
    wout[...] = term(c0[...], c1[...], og[0], og[1]).astype(wout.dtype)


def encode_back_kernel(n_mp, wemb, proj, *refs):
    parts = refs[:n_mp]
    grad, dproj, att_grad = refs[n_mp:]
    grad[...] = total(parts).astype(BF16)
    att_grad[...] = dot_t(grad[...], wemb[...]).astype(BF16)
    for g in groups_of(att_grad):
        dproj[0, :, g], dproj[1, :, g], dproj[2, :, g] = attention(
            proj[0, :, g], proj[1, :, g], proj[2, :, g], HD, up=att_grad[:, g], forward=False
        )


def seen_back_kernel(n_mp, vis, og, dec_in, wemb, proj, *refs):
    parts = (refs[:n_mp], refs[n_mp : 2 * n_mp])
    grad, dproj, att_grad = refs[2 * n_mp :]
    for j in range(2):
        sel = select_of(vis[j : j + 1, :])
        cot = total(parts[j])
        wide = dot(sel, dec_in[j])
        out = dot(sel, og[j])
        centred = wide - jnp.mean(wide, axis=-1, keepdims=True)
        inverse = lax.rsqrt(jnp.mean(centred * centred, axis=-1, keepdims=True) + EPS)
        unit = centred * inverse
        back = inverse * (
            cot
            - jnp.mean(cot, axis=-1, keepdims=True)
            - unit * jnp.mean(cot * unit, axis=-1, keepdims=True)
        )
        grad[j * VP : (j + 1) * VP, :] = (out + back).astype(BF16)
    att_grad[...] = dot_t(grad[...], wemb[...]).astype(BF16)
    mask = seen_mask(grad.shape[0])
    for g in groups_of(att_grad):
        dproj[0, :, g], dproj[1, :, g], dproj[2, :, g] = attention(
            proj[0, :, g], proj[1, :, g], proj[2, :, g], HD,
            up=att_grad[:, g], forward=False, mask=mask,
        )


def embed_weights_kernel(a0, a1, sa, g0, g1, sg, out):
    out[...] = (
        dot(flip(a0[...]).astype(BF16), g0[...])
        + dot(flip(a1[...]).astype(BF16), g1[...])
        + dot(flip(sa[...]).astype(BF16), sg[...])
    ).astype(out.dtype)


def encoder_weights_kernel(n0, n1, sn, d0, d1, sd, out):
    rows = 256
    for r in range(0, n0.shape[1], rows):
        cut = slice(r, r + rows)
        t0 = flip(n0[:, cut]).astype(BF16)
        t1 = flip(n1[:, cut]).astype(BF16)
        ts = flip(sn[:, cut]).astype(BF16)
        for c in range(3):
            out[c, cut, :] = (dot(t0, d0[c]) + dot(t1, d1[c]) + dot(ts, sd[c])).astype(out.dtype)


def exchange_kernel(n_full, n_streams, *refs):
    own = refs[:n_streams]
    outs = refs[n_streams : 2 * n_streams]
    scr = refs[2 * n_streams :]
    got_s = scr[:n_streams]
    sum_s = scr[n_streams : 2 * n_streams]
    got_a = scr[2 * n_streams : 3 * n_streams]
    sum_a = scr[3 * n_streams : 4 * n_streams]
    got_b = scr[4 * n_streams : 5 * n_streams]
    send, recv = scr[5 * n_streams :]
    s = lax.axis_index("side")
    p = lax.axis_index("pair")
    hi, lo = p // 2, p % 2
    to_s = {"side": 1 - s}
    to_a = {"pair": hi * 2 + 1 - lo}
    to_b = {"pair": (1 - hi) * 2 + lo}

    barrier = pltpu.get_barrier_semaphore()
    for to in (to_s, to_a, to_b):
        pl.semaphore_signal(barrier, inc=1, device_id=to, device_id_type=pl.DeviceIdType.MESH)
    pl.semaphore_wait(barrier, 3)

    def start(i, stage, src, dst, to):
        copy = pltpu.make_async_remote_copy(
            src_ref=src, dst_ref=dst, send_sem=send.at[i, stage], recv_sem=recv.at[i, stage],
            device_id=to, device_id_type=pl.DeviceIdType.MESH,
        )
        copy.start()
        return copy

    def add(a, b):
        return a.astype(F32) + b.astype(F32)

    stage_s = [start(i, 0, own[i].at[:, :, 1 - s], got_s[i], to_s) for i in range(n_streams)]
    stage_a, stage_b, gather = {}, {}, {}

    def run_a(i):
        stage_s[i].wait()
        for h in range(2):
            for l in range(2):
                sum_s[i][h, l] = add(own[i][h, l, s], got_s[i][h, l]).astype(BF16)
        stage_a[i] = start(i, 1, sum_s[i].at[:, 1 - lo], got_a[i], to_a)

    def run_b(i):
        stage_a[i].wait()
        for h in range(2):
            sum_a[i][h] = add(sum_s[i][h, lo], got_a[i][h]).astype(BF16)
        stage_b[i] = start(i, 2, sum_a[i].at[1 - hi], got_b[i], to_b)

    def run_sum(i):
        stage_b[i].wait()
        block = add(sum_a[i][hi], got_b[i][...]).astype(outs[i].dtype)
        if i < n_full:
            outs[i][hi, lo, s] = block
            mine = outs[i].at[hi, lo, s]
            gather[i] = start(i, 3, mine, mine, to_b)
        else:
            outs[i][...] = block

    def run_g1(i):
        gather[i].wait()
        mine = outs[i].at[:, lo, s]
        gather[i] = start(i, 4, mine, mine, to_a)

    def run_g2(i):
        gather[i].wait()
        mine = outs[i].at[:, :, s]
        gather[i] = start(i, 5, mine, mine, to_s)

    full, rest = list(range(n_full)), list(range(n_full, n_streams))
    for i in full + rest:
        run_a(i)
    for i in full:
        run_b(i)
    later = [run_sum, run_g1, run_g2]
    for step, i in enumerate(rest):
        run_b(i)
        if step < len(later):
            for f in full:
                later[step](f)
    for f in later[len(rest):]:
        for i in full:
            f(i)
    for i in rest:
        run_sum(i)
    for i in full:
        gather[i].wait()


def exchange(full, rest):
    arrays = full + rest
    n = len(arrays)
    tails = [a.shape[3:] for a in arrays]
    outs = [(a.shape if i < len(full) else a.shape[3:], BF16) for i, a in enumerate(arrays)]
    scratch = []
    for lead in ((2, 2), (2, 2), (2,), (2,), ()):
        scratch += [pltpu.VMEM(lead + t, BF16) for t in tails]
    return pl.pallas_call(
        functools.partial(exchange_kernel, len(full), n),
        out_shape=[jax.ShapeDtypeStruct(sh, t) for sh, t in outs],
        in_specs=[pl.BlockSpec(memory_space=pltpu.VMEM)] * n,
        out_specs=[pl.BlockSpec(memory_space=pltpu.VMEM)] * n,
        scratch_shapes=scratch
        + [pltpu.SemaphoreType.DMA((n, 6)), pltpu.SemaphoreType.DMA((n, 6))],
        compiler_params=pltpu.CompilerParams(
            vmem_limit_bytes=VMEM_LIMIT, collective_id=0, has_side_effects=True
        ),
    )(*arrays)


def widen_kernel(a0, a1, a2, c0, c1, c2, b0, b1, b2, out):
    for a, b in ((a0, b0), (a1, b1), (a2, b2)):
        b[...] = a[...].astype(F32)
    for c, a in enumerate((c0, c1, c2)):
        out[c] = a[...].astype(F32)


def call(kernel, outs, args, scratch=(), smem=0, flops=0):
    specs = [pl.BlockSpec(memory_space=pltpu.SMEM)] * smem
    specs += [pl.BlockSpec(memory_space=pltpu.VMEM)] * (len(args) - smem)
    bytes_moved = sum(a.size * a.dtype.itemsize for a in args) + sum(
        math.prod(s) * jnp.dtype(t).itemsize for s, t in outs
    )
    return pl.pallas_call(
        kernel,
        out_shape=[jax.ShapeDtypeStruct(s, t) for s, t in outs],
        in_specs=specs,
        out_specs=[pl.BlockSpec(memory_space=pltpu.VMEM)] * len(outs),
        scratch_shapes=[pltpu.VMEM(s, t) for s, t in scratch],
        compiler_params=pltpu.CompilerParams(vmem_limit_bytes=VMEM_LIMIT),
        cost_estimate=pl.CostEstimate(
            flops=flops, bytes_accessed=bytes_moved, transcendentals=0
        ),
    )(*args)


def shifted(x, axis, k):
    n = lax.axis_size(axis)
    return lax.ppermute(x, axis, [(i, (i + k) % n) for i in range(n)])


def all_parts(x):
    return [x] + [shifted(x, "mp", k) for k in range(1, lax.axis_size("mp"))]


def body(past, future, visible, partner, wenc, wemb, mask_token, pos, wqkv, wout, og):
    frames, np_, width = past.shape
    dd = pos.shape[1]
    n_mp = lax.axis_size("mp")
    half = lax.axis_size("pair") // 2
    ew, dw = wenc.shape[2], wqkv.shape[2]
    big = 6_000_000_000

    me = lax.axis_index("mp")
    where = (me - jnp.arange(n_mp, dtype=jnp.int32)) % n_mp
    wanted = shifted(partner, "pair", half)[0]
    span = width // n_mp
    strip = lax.dynamic_slice_in_dim(past, me * span, span, axis=2)
    strips = [jnp.where(wanted[j] == 0, strip[0], strip[1]) for j in range(frames)]

    sr = frames * VP
    seen_normed, seen_proj, seen_att, seen_part = call(
        seen_kernel,
        [((sr, width), BF16), ((3, sr, ew), BF16), ((sr, ew), BF16), ((sr, dd), BF16)],
        (future, visible, wenc, wemb), flops=big // 4,
    )
    early = shifted(strips[0], "pair", half)
    late, seen_part = lax.optimization_barrier((strips[1], seen_part))
    late = shifted(late, "pair", half)
    arrived = [all_parts(early), all_parts(late)]
    dec_in, normed_dec, query, cgrad = call(
        functools.partial(query_kernel, n_mp),
        [((frames, np_, dd), BF16)] * 2 + [((frames, np_, dw), BF16)] * 2,
        (visible, mask_token.reshape(1, dd), pos, wqkv, wout, og, *all_parts(seen_part)),
        flops=big // 4,
    )
    enc = [
        call(
            functools.partial(encode_kernel, n_mp),
            [((np_, width), BF16), ((3, np_, ew), BF16), ((np_, ew), BF16), ((np_, dd), BF16)],
            (where, *arrived[j], wenc, wemb), smem=1, flops=big,
            scratch=[((np_, width), BF16)],
        )
        for j in range(frames)
    ]
    emb_parts = [all_parts(e[3]) for e in enc]
    dec = [
        call(
            functools.partial(decode_kernel, j, n_mp),
            [((np_, dd), BF16)] + [((np_, dw), BF16)] * 4
            + [((np_, dd), BF16)] * 2 + [((VP, dd), BF16)],
            (visible, pos, wqkv, wout, query, cgrad, *emb_parts[j]),
            scratch=[((np_, dw), BF16)] * 2, flops=big,
        )
        for j in range(frames)
    ]
    paired, ctx, dq, dk, dv, update, pair_part, vis_part = zip(*dec)
    pair_parts = [all_parts(x) for x in pair_part]
    vis_parts = [all_parts(x) for x in vis_part]
    updates = [all_parts(x) for x in update]
    qkv_term, out_term = call(
        decoder_weights_kernel,
        [(wqkv.shape, BF16), (wout.shape, BF16)],
        (normed_dec, og, *paired, *ctx, *dq, *dk, *dv), flops=big // 2,
    )
    seen_grad, seen_dproj = call(
        functools.partial(seen_back_kernel, n_mp),
        [((sr, dd), BF16), ((3, sr, ew), BF16)],
        (visible, og, dec_in, wemb, seen_proj, *vis_parts[0], *vis_parts[1]),
        scratch=[((sr, ew), BF16)], flops=big // 4,
    )
    back = [
        call(
            functools.partial(encode_back_kernel, n_mp),
            [((np_, dd), BF16), ((3, np_, ew), BF16)],
            (wemb, enc[j][1], *pair_parts[j]),
            scratch=[((np_, ew), BF16)], flops=big,
        )
        for j in range(frames)
    ]
    (embed_term,) = call(
        embed_weights_kernel, [(wemb.shape, BF16)],
        (enc[0][2], enc[1][2], seen_att, back[0][0], back[1][0], seen_grad), flops=big // 4,
    )
    (enc_term,) = call(
        encoder_weights_kernel, [(wenc.shape, BF16)],
        (enc[0][0], enc[1][0], seen_normed, back[0][1], back[1][1], seen_dproj), flops=big,
    )
    prediction = jnp.stack([
        (dec_in[j].astype(F32) + sum(u.astype(F32) for u in updates[j])).astype(BF16)
        for j in range(frames)
    ])
    if lax.axis_size("pair") == 4:
        ds = [embed_term, qkv_term.reshape(-1, dw), out_term]
        bits = [x.reshape(2, 2, 2, x.shape[0] // 8, x.shape[1]) for x in ds]
        cs = [enc_term[c].reshape(2, 2, 2, width // 8, ew) for c in range(3)]
        sums = exchange(bits, cs)
        shapes = [wemb.shape, (3 * dd, dw), wout.shape]
        dense = [x.reshape(sh) for x, sh in zip(sums[:3], shapes)]
        wide = call(
            widen_kernel,
            [(x.shape, F32) for x in dense] + [((3, width // 8, ew), F32)],
            (*dense, *sums[3:]),
        )
        embed_grad, qkv_grad, out_grad = wide[0], wide[1].reshape(wqkv.shape), wide[2]
        enc_grad = wide[3]
    else:
        enc_grad = lax.psum_scatter(
            enc_term, ("pair", "side"), scatter_dimension=1, tiled=True
        ).astype(F32)
        embed_grad, qkv_grad, out_grad = (
            x.astype(F32)
            for x in lax.psum((embed_term, qkv_term, out_term), ("pair", "side"))
        )
    return (prediction, enc_grad, embed_grad, qkv_grad, out_grad)


def solution(mesh):
    rows = ("groups", "pair", "side")
    in_specs = (
        P(rows, None, None),
        P(rows, None, None),
        P(rows, None),
        P(rows, None),
        P(None, None, "mp"),
        P("mp", None),
        P(),
        P(),
        P(None, None, "mp"),
        P("mp", None),
        P(rows, None, None),
    )
    out_specs = (
        P(rows, None, None),
        P("groups", ("pair", "side"), "mp"),
        P(("groups", "mp"), None),
        P("groups", None, "mp"),
        P(("groups", "mp"), None),
    )
    return jax.shard_map(body, mesh=mesh, in_specs=in_specs, out_specs=out_specs, check_vma=False)
```

```python
import functools
import math

import jax
import jax.numpy as jnp
from jax import lax
from jax.experimental import pallas as pl
from jax.experimental.pallas import tpu as pltpu
from jax.sharding import PartitionSpec as P

VIS = 10
VP = 16
HD = 64
DHD = 32
EPS = 1e-06
F32 = jnp.float32
BF16 = jnp.bfloat16
VMEM_LIMIT = 56 * 1024 * 1024


def dot(a, b):
    return jnp.dot(a, b, preferred_element_type=F32)


def dot_t(a, b):
    return lax.dot_general(a, b, (((1,), (1,)), ((), ())), preferred_element_type=F32)


def flip(a):
    return a.astype(F32).T


def normalize(wide):
    centred = wide - jnp.mean(wide, axis=-1, keepdims=True)
    return centred * lax.rsqrt(jnp.mean(centred * centred, axis=-1, keepdims=True) + EPS)


def softmax(scores):
    e = jnp.exp(scores - jnp.max(scores, axis=-1, keepdims=True))
    return e * (1.0 / jnp.sum(e, axis=-1, keepdims=True))


def head_cols(h, hs, x):
    lane = lax.broadcasted_iota(jnp.int32, x.shape, 1)
    return jnp.where((lane >= h * hs) & (lane < (h + 1) * hs), x, jnp.zeros_like(x))


def attention(q, k, v, hs, up=None, forward=True, mask=None):
    scale = 1.0 / math.sqrt(hs)
    ctx = dq = None
    dkt, dvt = [], []
    if up is not None:
        upt = flip(up).astype(BF16)
        qt = flip(q).astype(BF16)
    for h in range(q.shape[1] // hs):
        s = dot_t(head_cols(h, hs, q), k) * scale
        if mask is not None:
            s = jnp.where(mask, s, -1e30)
        p = softmax(s)
        w = p.astype(BF16)
        if forward:
            c = dot(w, head_cols(h, hs, v))
            ctx = c if ctx is None else ctx + c
        if up is not None:
            dp = dot_t(head_cols(h, hs, up), v)
            dvt.append(dot(upt[h * hs : (h + 1) * hs], w))
            ds = (p * (dp - jnp.sum(dp * p, axis=-1, keepdims=True)) * scale).astype(BF16)
            d = dot(ds, head_cols(h, hs, k))
            dq = d if dq is None else dq + d
            dkt.append(dot(qt[h * hs : (h + 1) * hs], ds))
    out = []
    if forward:
        out.append(ctx.astype(BF16))
    if up is not None:
        out += [
            dq.astype(BF16),
            jnp.concatenate(dkt, 0).T.astype(BF16),
            jnp.concatenate(dvt, 0).T.astype(BF16),
        ]
    return out


def groups_of(ref):
    n = ref.shape[-1]
    return [slice(i, i + 128) for i in range(0, n, 128)]


def select_of(visible):
    n = visible.shape[1]
    lower = lax.broadcasted_iota(jnp.int32, (n, n), 0) <= lax.broadcasted_iota(jnp.int32, (n, n), 1)
    rank = dot(visible.astype(F32).astype(BF16), lower.astype(F32).astype(BF16))
    row = lax.broadcasted_iota(jnp.int32, (VP, n), 0).astype(F32) + 1.0
    picks = (row == rank) & (visible.astype(F32) > 0.5)
    return picks.astype(F32).astype(BF16)


def total(refs, index=None):
    acc = None
    for r in refs:
        x = (r[...] if index is None else r[index]).astype(F32)
        acc = x if acc is None else acc + x
    return acc


def seen_mask(rows):
    a = lax.broadcasted_iota(jnp.int32, (rows, rows), 0)
    b = lax.broadcasted_iota(jnp.int32, (rows, rows), 1)
    return (a // VP == b // VP) & (b % VP < VIS)


def seen_kernel(fut, vis, wenc, wemb, normed, proj, att, part):
    for j in range(fut.shape[0]):
        sel = select_of(vis[j : j + 1, :])
        seen = dot(sel, fut[j]).astype(BF16)
        normed[j * VP : (j + 1) * VP, :] = normalize(seen.astype(F32)).astype(BF16)
    x = normed[...]
    for c in range(3):
        proj[c] = dot(x, wenc[c]).astype(BF16)
    mask = seen_mask(x.shape[0])
    for g in groups_of(att):
        (att[:, g],) = attention(proj[0, :, g], proj[1, :, g], proj[2, :, g], HD, mask=mask)
    part[...] = dot(att[...], wemb[...]).astype(BF16)


def query_kernel(n_mp, vis, mask_token, pos, wq, wout, og, *refs):
    parts = refs[:n_mp]
    dec_in, normed, query, cgrad = refs[n_mp:]
    for j in range(og.shape[0]):
        v = vis[j : j + 1, :]
        sel = select_of(v)
        emb = total(parts, (slice(j * VP, (j + 1) * VP), slice(None))).astype(BF16)
        placed = dot(flip(sel).astype(BF16), emb)
        hidden = 1.0 - flip(jnp.broadcast_to(v, (8, v.shape[1])))[:, :1]
        d = (placed + hidden * mask_token[...].astype(F32) + pos[...].astype(F32)).astype(BF16)
        dec_in[j] = d
        x = normalize(d.astype(F32)).astype(BF16)
        normed[j] = x
        query[j] = dot(x, wq[0]).astype(BF16)
        cgrad[j] = dot_t(og[j], wout[...]).astype(BF16)


def encode_kernel(n_mp, where, *refs):
    parts = refs[:n_mp]
    wenc, wemb, normed, proj, att, part, whole = refs[n_mp:]
    span = parts[0].shape[1]
    for k in range(n_mp):
        whole[:, pl.ds(pl.multiple_of(where[k] * span, span), span)] = parts[k][...]
    normed[...] = normalize(whole[...].astype(F32)).astype(BF16)
    for c in range(3):
        proj[c] = dot(normed[...], wenc[c]).astype(BF16)
    for g in groups_of(att):
        (att[:, g],) = attention(proj[0, :, g], proj[1, :, g], proj[2, :, g], HD)
    part[...] = dot(att[...], wemb[...]).astype(BF16)


def decode_kernel(j, n_mp, vis, pos, wqkv, wout, query, cgrad, *refs):
    parts = refs[:n_mp]
    paired, ctx, dq, dk, dv, update, pair_part, vis_part, keys, values = refs[n_mp:]
    emb = total(parts).astype(BF16)
    paired[...] = (emb.astype(F32) + pos[...].astype(F32)).astype(BF16)
    keys[...] = dot(paired[...], wqkv[1]).astype(BF16)
    values[...] = dot(paired[...], wqkv[2]).astype(BF16)
    for g in groups_of(ctx):
        ctx[:, g], dq[:, g], dk[:, g], dv[:, g] = attention(
            query[j, :, g], keys[:, g], values[:, g], DHD, up=cgrad[j, :, g]
        )
    pair_part[...] = (dot_t(dk[...], wqkv[1]) + dot_t(dv[...], wqkv[2])).astype(BF16)
    chosen = dot(select_of(vis[j : j + 1, :]), dq[...]).astype(BF16)
    vis_part[...] = dot_t(chosen, wqkv[0]).astype(BF16)
    update[...] = dot(ctx[...], wout[...]).astype(BF16)


def decoder_weights_kernel(normed, og, p0, p1, c0, c1, q0, q1, k0, k1, v0, v1, qkv, wout):
    def term(a0, a1, b0, b1):
        return dot(flip(a0).astype(BF16), b0) + dot(flip(a1).astype(BF16), b1)

    qkv[0] = term(normed[0], normed[1], q0[...], q1[...]).astype(qkv.dtype)
    pt0, pt1 = flip(p0[...]).astype(BF16), flip(p1[...]).astype(BF16)
    qkv[1] = (dot(pt0, k0[...]) + dot(pt1, k1[...])).astype(qkv.dtype)
    qkv[2] = (dot(pt0, v0[...]) + dot(pt1, v1[...])).astype(qkv.dtype)
    wout[...] = term(c0[...], c1[...], og[0], og[1]).astype(wout.dtype)


def encode_back_kernel(n_mp, wemb, proj, *refs):
    parts = refs[:n_mp]
    grad, dproj, att_grad = refs[n_mp:]
    grad[...] = total(parts).astype(BF16)
    att_grad[...] = dot_t(grad[...], wemb[...]).astype(BF16)
    for g in groups_of(att_grad):
        dproj[0, :, g], dproj[1, :, g], dproj[2, :, g] = attention(
            proj[0, :, g], proj[1, :, g], proj[2, :, g], HD, up=att_grad[:, g], forward=False
        )


def seen_back_kernel(n_mp, vis, og, dec_in, wemb, proj, *refs):
    parts = (refs[:n_mp], refs[n_mp : 2 * n_mp])
    grad, dproj, att_grad = refs[2 * n_mp :]
    for j in range(2):
        sel = select_of(vis[j : j + 1, :])
        cot = total(parts[j])
        wide = dot(sel, dec_in[j])
        out = dot(sel, og[j])
        centred = wide - jnp.mean(wide, axis=-1, keepdims=True)
        inverse = lax.rsqrt(jnp.mean(centred * centred, axis=-1, keepdims=True) + EPS)
        unit = centred * inverse
        back = inverse * (
            cot
            - jnp.mean(cot, axis=-1, keepdims=True)
            - unit * jnp.mean(cot * unit, axis=-1, keepdims=True)
        )
        grad[j * VP : (j + 1) * VP, :] = (out + back).astype(BF16)
    att_grad[...] = dot_t(grad[...], wemb[...]).astype(BF16)
    mask = seen_mask(grad.shape[0])
    for g in groups_of(att_grad):
        dproj[0, :, g], dproj[1, :, g], dproj[2, :, g] = attention(
            proj[0, :, g], proj[1, :, g], proj[2, :, g], HD,
            up=att_grad[:, g], forward=False, mask=mask,
        )


def embed_weights_kernel(a0, a1, sa, g0, g1, sg, out):
    out[...] = (
        dot(flip(a0[...]).astype(BF16), g0[...])
        + dot(flip(a1[...]).astype(BF16), g1[...])
        + dot(flip(sa[...]).astype(BF16), sg[...])
    ).astype(out.dtype)


def encoder_weights_kernel(n0, n1, sn, d0, d1, sd, out):
    rows = 256
    for r in range(0, n0.shape[1], rows):
        cut = slice(r, r + rows)
        t0 = flip(n0[:, cut]).astype(BF16)
        t1 = flip(n1[:, cut]).astype(BF16)
        ts = flip(sn[:, cut]).astype(BF16)
        for c in range(3):
            out[c, cut, :] = (dot(t0, d0[c]) + dot(t1, d1[c]) + dot(ts, sd[c])).astype(out.dtype)


def tail_kernel(n_mp, n_groups, *refs):
    n = 3 + n_groups
    n_full = 3
    (qkv_own, out_own, wemb, proj0, proj1, att0, att1, seen_att, seen_grad, seen_dproj,
     n0, n1, sn) = refs[:13]
    refs = refs[13:]
    parts = (refs[:n_mp], refs[n_mp : 2 * n_mp])
    refs = refs[2 * n_mp :]
    outs = refs[:n]
    refs = refs[n:]
    emb_own, *enc_own = refs[: 1 + n_groups]
    refs = refs[1 + n_groups :]
    own = [qkv_own, out_own, emb_own, *enc_own]
    got_s, sum_s, got_a, sum_a, got_b = (refs[k * n : (k + 1) * n] for k in range(5))
    grads, att_grads, flipped, seen_flipped, send, recv = (
        refs[5 * n : 5 * n + 2], refs[5 * n + 2 : 5 * n + 4], refs[5 * n + 4 : 5 * n + 6],
        refs[5 * n + 6], refs[5 * n + 7], refs[5 * n + 8],
    )
    s = lax.axis_index("side")
    p = lax.axis_index("pair")
    hi, lo = p // 2, p % 2
    to_s = {"side": 1 - s}
    to_a = {"pair": hi * 2 + 1 - lo}
    to_b = {"pair": (1 - hi) * 2 + lo}

    barrier = pltpu.get_barrier_semaphore()
    for to in (to_s, to_a, to_b):
        pl.semaphore_signal(barrier, inc=1, device_id=to, device_id_type=pl.DeviceIdType.MESH)
    pl.semaphore_wait(barrier, 3)

    def start(i, stage, src, dst, to):
        copy = pltpu.make_async_remote_copy(
            src_ref=src, dst_ref=dst, send_sem=send.at[i, stage], recv_sem=recv.at[i, stage],
            device_id=to, device_id_type=pl.DeviceIdType.MESH,
        )
        copy.start()
        return copy

    def add(a, b):
        return a.astype(F32) + b.astype(F32)

    stage_s, stage_a, stage_b, gather = {}, {}, {}, {}

    def run_s(i):
        stage_s[i] = start(i, 0, own[i].at[:, :, 1 - s], got_s[i], to_s)

    def run_a(i):
        stage_s[i].wait()
        for h in range(2):
            for l in range(2):
                sum_s[i][h, l] = add(own[i][h, l, s], got_s[i][h, l]).astype(BF16)
        stage_a[i] = start(i, 1, sum_s[i].at[:, 1 - lo], got_a[i], to_a)

    def run_b(i):
        stage_a[i].wait()
        for h in range(2):
            sum_a[i][h] = add(sum_s[i][h, lo], got_a[i][h]).astype(BF16)
        stage_b[i] = start(i, 2, sum_a[i].at[1 - hi], got_b[i], to_b)

    def run_sum(i):
        stage_b[i].wait()
        block = add(sum_a[i][hi], got_b[i][...]).astype(outs[i].dtype)
        if i < n_full:
            outs[i][hi, lo, s] = block
            mine = outs[i].at[hi, lo, s]
            gather[i] = start(i, 3, mine, mine, to_b)
        else:
            outs[i][...] = block

    def run_g1(i):
        gather[i].wait()
        mine = outs[i].at[:, lo, s]
        gather[i] = start(i, 4, mine, mine, to_a)

    def run_g2(i):
        gather[i].wait()
        mine = outs[i].at[:, :, s]
        gather[i] = start(i, 5, mine, mine, to_s)

    def run_end(i):
        gather[i].wait()

    def blocks():
        return [(h, l, t) for h in range(2) for l in range(2) for t in range(2)]

    run_s(0)
    run_s(1)
    for j in range(2):
        grads[j][...] = total(parts[j]).astype(BF16)
    emb_rows = emb_own.shape[3]
    term = (
        dot(flip(att0[...]).astype(BF16), grads[0][...])
        + dot(flip(att1[...]).astype(BF16), grads[1][...])
        + dot(flip(seen_att[...]).astype(BF16), seen_grad[...])
    ).astype(BF16)
    for k, (h, l, t) in enumerate(blocks()):
        emb_own[h, l, t] = term[k * emb_rows : (k + 1) * emb_rows]
    run_s(2)
    run_a(0)
    run_a(1)
    for j in range(2):
        att_grads[j][...] = dot_t(grads[j][...], wemb[...]).astype(BF16)
    depth = n0.shape[1]
    step = depth // 4
    for r in range(0, depth, step):
        flipped[0][r : r + step, :] = flip(n0[:, r : r + step]).astype(BF16)
        flipped[1][r : r + step, :] = flip(n1[:, r : r + step]).astype(BF16)
        seen_flipped[r : r + step, :] = flip(sn[:, r : r + step]).astype(BF16)
    run_a(2)

    later = {k: [] for k in range(n_groups + 6)}

    def plan(i, at, first):
        stages = [run_a, run_b, run_sum, run_g1, run_g2, run_end][first:]
        for k, f in enumerate(stages if i < n_full else stages[: 3 - first]):
            later[min(at + k, n_groups + 5)].append(functools.partial(f, i))

    for g in range(n_groups):
        plan(n_full + g, g + 1, 0)
    for i in (0, 1):
        plan(i, 0, 1)
    plan(2, 1, 1)

    eighth = depth // 8
    for g in range(n_groups):
        cut = slice(g * 128, (g + 1) * 128)
        both = []
        for j, proj in enumerate((proj0, proj1)):
            d = attention(
                proj[0, :, cut], proj[1, :, cut], proj[2, :, cut], HD,
                up=att_grads[j][:, cut], forward=False,
            )
            both.append(jnp.concatenate(d, 1))
        seen_d = jnp.concatenate([seen_dproj[c, :, cut] for c in range(3)], 1)
        for k, (h, l, t) in enumerate(blocks()):
            rows = slice(k * eighth, (k + 1) * eighth)
            block = (
                dot(flipped[0][rows, :], both[0])
                + dot(flipped[1][rows, :], both[1])
                + dot(seen_flipped[rows, :], seen_d)
            ).astype(BF16)
            for c in range(3):
                enc_own[g][h, l, t, c * eighth : (c + 1) * eighth, :] = block[
                    :, c * 128 : (c + 1) * 128
                ]
        run_s(n_full + g)
        for f in later[g]:
            f()
    for k in range(n_groups, n_groups + 6):
        for f in later[k]:
            f()


def tail(qkv_term, out_term, args, parts0, parts1):
    wemb, np_, depth, ew = args[0], args[1].shape[1], args[8].shape[1], args[1].shape[2]
    n_groups = ew // 128
    eight = (2, 2, 2)
    emb_tail = (wemb.shape[0] // 8, wemb.shape[1])
    enc_tail = (3 * depth // 8, 128)
    tails = [qkv_term.shape[3:], out_term.shape[3:], emb_tail] + [enc_tail] * n_groups
    outs = [(eight + t) for t in tails[:3]] + tails[3:]
    scratch = [pltpu.VMEM(eight + t, BF16) for t in tails[2:]]
    for lead in ((2, 2), (2, 2), (2,), (2,), ()):
        scratch += [pltpu.VMEM(lead + t, BF16) for t in tails]
    dd, sr = wemb.shape[1], args[7].shape[1]
    n = len(tails)
    scratch += [pltpu.VMEM((np_, dd), BF16)] * 2 + [pltpu.VMEM((np_, ew), BF16)] * 2
    scratch += [pltpu.VMEM((depth, np_), BF16)] * 2 + [pltpu.VMEM((depth, sr), BF16)]
    scratch += [pltpu.SemaphoreType.DMA((n, 6))] * 2
    operands = (qkv_term, out_term, *args, *parts0, *parts1)
    return pl.pallas_call(
        functools.partial(tail_kernel, len(parts0), n_groups),
        out_shape=[jax.ShapeDtypeStruct(sh, BF16) for sh in outs],
        in_specs=[pl.BlockSpec(memory_space=pltpu.VMEM)] * len(operands),
        out_specs=[pl.BlockSpec(memory_space=pltpu.VMEM)] * n,
        scratch_shapes=scratch,
        compiler_params=pltpu.CompilerParams(
            vmem_limit_bytes=VMEM_LIMIT, collective_id=0, has_side_effects=True
        ),
    )(*operands)


def widen_kernel(n_groups, *refs):
    ins, outs = refs[: 3 + n_groups], refs[3 + n_groups :]
    for a, b in zip(ins[:3], outs[:3]):
        b[...] = a[...].astype(F32)
    rows = outs[3].shape[1]
    for g, a in enumerate(ins[3:]):
        for c in range(3):
            outs[3][c, :, g * 128 : (g + 1) * 128] = a[c * rows : (c + 1) * rows, :].astype(F32)


def call(kernel, outs, args, scratch=(), smem=0, flops=0):
    specs = [pl.BlockSpec(memory_space=pltpu.SMEM)] * smem
    specs += [pl.BlockSpec(memory_space=pltpu.VMEM)] * (len(args) - smem)
    bytes_moved = sum(a.size * a.dtype.itemsize for a in args) + sum(
        math.prod(s) * jnp.dtype(t).itemsize for s, t in outs
    )
    return pl.pallas_call(
        kernel,
        out_shape=[jax.ShapeDtypeStruct(s, t) for s, t in outs],
        in_specs=specs,
        out_specs=[pl.BlockSpec(memory_space=pltpu.VMEM)] * len(outs),
        scratch_shapes=[pltpu.VMEM(s, t) for s, t in scratch],
        compiler_params=pltpu.CompilerParams(vmem_limit_bytes=VMEM_LIMIT),
        cost_estimate=pl.CostEstimate(
            flops=flops, bytes_accessed=bytes_moved, transcendentals=0
        ),
    )(*args)


def shifted(x, axis, k):
    n = lax.axis_size(axis)
    return lax.ppermute(x, axis, [(i, (i + k) % n) for i in range(n)])


def all_parts(x):
    return [x] + [shifted(x, "mp", k) for k in range(1, lax.axis_size("mp"))]


def body(past, future, visible, partner, wenc, wemb, mask_token, pos, wqkv, wout, og):
    frames, np_, width = past.shape
    dd = pos.shape[1]
    n_mp = lax.axis_size("mp")
    half = lax.axis_size("pair") // 2
    ew, dw = wenc.shape[2], wqkv.shape[2]
    big = 6_000_000_000

    me = lax.axis_index("mp")
    where = (me - jnp.arange(n_mp, dtype=jnp.int32)) % n_mp
    wanted = shifted(partner, "pair", half)[0]
    span = width // n_mp
    strip = lax.dynamic_slice_in_dim(past, me * span, span, axis=2)
    strips = [jnp.where(wanted[j] == 0, strip[0], strip[1]) for j in range(frames)]

    first, future = lax.optimization_barrier((strips[0], future))
    early = shifted(first, "pair", half)
    sr = frames * VP
    seen_normed, seen_proj, seen_att, seen_part = call(
        seen_kernel,
        [((sr, width), BF16), ((3, sr, ew), BF16), ((sr, ew), BF16), ((sr, dd), BF16)],
        (future, visible, wenc, wemb), flops=big // 4,
    )
    late, seen_part = lax.optimization_barrier((strips[1], seen_part))
    late = shifted(late, "pair", half)
    arrived = [all_parts(early), all_parts(late)]
    dec_in, normed_dec, query, cgrad = call(
        functools.partial(query_kernel, n_mp),
        [((frames, np_, dd), BF16)] * 2 + [((frames, np_, dw), BF16)] * 2,
        (visible, mask_token.reshape(1, dd), pos, wqkv, wout, og, *all_parts(seen_part)),
        flops=big // 4,
    )
    arrived[0][0], query = lax.optimization_barrier((arrived[0][0], query))
    enc = [
        call(
            functools.partial(encode_kernel, n_mp),
            [((np_, width), BF16), ((3, np_, ew), BF16), ((np_, ew), BF16), ((np_, dd), BF16)],
            (where, *arrived[j], wenc, wemb), smem=1, flops=big,
            scratch=[((np_, width), BF16)],
        )
        for j in range(frames)
    ]
    emb_parts = [all_parts(e[3]) for e in enc]
    dec = [
        call(
            functools.partial(decode_kernel, j, n_mp),
            [((np_, dd), BF16)] + [((np_, dw), BF16)] * 4
            + [((np_, dd), BF16)] * 2 + [((VP, dd), BF16)],
            (visible, pos, wqkv, wout, query, cgrad, *emb_parts[j]),
            scratch=[((np_, dw), BF16)] * 2, flops=big,
        )
        for j in range(frames)
    ]
    paired, ctx, dq, dk, dv, update, pair_part, vis_part = zip(*dec)
    pair_parts = [all_parts(x) for x in pair_part]
    vis_parts = [all_parts(x) for x in vis_part]
    updates = [all_parts(x) for x in update]
    qkv_term, out_term = call(
        decoder_weights_kernel,
        [(wqkv.shape, BF16), (wout.shape, BF16)],
        (normed_dec, og, *paired, *ctx, *dq, *dk, *dv), flops=big // 2,
    )
    seen_grad, seen_dproj = call(
        functools.partial(seen_back_kernel, n_mp),
        [((sr, dd), BF16), ((3, sr, ew), BF16)],
        (visible, og, dec_in, wemb, seen_proj, *vis_parts[0], *vis_parts[1]),
        scratch=[((sr, ew), BF16)], flops=big // 4,
    )
    prediction = jnp.stack([
        (dec_in[j].astype(F32) + sum(u.astype(F32) for u in updates[j])).astype(BF16)
        for j in range(frames)
    ])
    if lax.axis_size("pair") == 4:
        def split(x):
            return x.reshape(2, 2, 2, x.shape[0] // 8, x.shape[1])

        sums = tail(
            split(qkv_term.reshape(-1, dw)), split(out_term),
            (wemb, enc[0][1], enc[1][1], enc[0][2], enc[1][2], seen_att, seen_grad, seen_dproj,
             enc[0][0], enc[1][0], seen_normed),
            pair_parts[0], pair_parts[1],
        )
        shapes = [(3 * dd, dw), wout.shape, wemb.shape]
        dense = [x.reshape(sh) for x, sh in zip(sums[:3], shapes)]
        qkv_grad, out_grad, embed_grad, enc_grad = call(
            functools.partial(widen_kernel, ew // 128),
            [(x.shape, F32) for x in dense] + [((3, width // 8, ew), F32)],
            (*dense, *sums[3:]),
        )
        qkv_grad = qkv_grad.reshape(wqkv.shape)
    else:
        back = [
            call(
                functools.partial(encode_back_kernel, n_mp),
                [((np_, dd), BF16), ((3, np_, ew), BF16)],
                (wemb, enc[j][1], *pair_parts[j]),
                scratch=[((np_, ew), BF16)], flops=big,
            )
            for j in range(frames)
        ]
        (embed_term,) = call(
            embed_weights_kernel, [(wemb.shape, BF16)],
            (enc[0][2], enc[1][2], seen_att, back[0][0], back[1][0], seen_grad), flops=big // 4,
        )
        (enc_term,) = call(
            encoder_weights_kernel, [(wenc.shape, BF16)],
            (enc[0][0], enc[1][0], seen_normed, back[0][1], back[1][1], seen_dproj), flops=big,
        )
        enc_grad = lax.psum_scatter(
            enc_term, ("pair", "side"), scatter_dimension=1, tiled=True
        ).astype(F32)
        embed_grad, qkv_grad, out_grad = (
            x.astype(F32)
            for x in lax.psum((embed_term, qkv_term, out_term), ("pair", "side"))
        )
    return (prediction, enc_grad, embed_grad, qkv_grad, out_grad)


def solution(mesh):
    rows = ("groups", "pair", "side")
    in_specs = (
        P(rows, None, None),
        P(rows, None, None),
        P(rows, None),
        P(rows, None),
        P(None, None, "mp"),
        P("mp", None),
        P(),
        P(),
        P(None, None, "mp"),
        P("mp", None),
        P(rows, None, None),
    )
    out_specs = (
        P(rows, None, None),
        P("groups", ("pair", "side"), "mp"),
        P(("groups", "mp"), None),
        P("groups", None, "mp"),
        P(("groups", "mp"), None),
    )
    return jax.shard_map(body, mesh=mesh, in_specs=in_specs, out_specs=out_specs, check_vma=False)
```

```python
import functools
import math

import jax
import jax.numpy as jnp
from jax import lax
from jax.experimental import pallas as pl
from jax.experimental.pallas import tpu as pltpu
from jax.sharding import PartitionSpec as P

VIS = 10
VP = 16
HD = 64
DHD = 32
EPS = 1e-06
F32 = jnp.float32
BF16 = jnp.bfloat16
VMEM_LIMIT = 56 * 1024 * 1024


def dot(a, b):
    return jnp.dot(a, b, preferred_element_type=F32)


def dot_t(a, b):
    return lax.dot_general(a, b, (((1,), (1,)), ((), ())), preferred_element_type=F32)


def flip(a):
    return a.astype(F32).T


def normalize(wide):
    centred = wide - jnp.mean(wide, axis=-1, keepdims=True)
    return centred * lax.rsqrt(jnp.mean(centred * centred, axis=-1, keepdims=True) + EPS)


def softmax(scores):
    e = jnp.exp(scores - jnp.max(scores, axis=-1, keepdims=True))
    return e * (1.0 / jnp.sum(e, axis=-1, keepdims=True))


def head_cols(h, hs, x):
    lane = lax.broadcasted_iota(jnp.int32, x.shape, 1)
    return jnp.where((lane >= h * hs) & (lane < (h + 1) * hs), x, jnp.zeros_like(x))


def attention(q, k, v, hs, up=None, forward=True, mask=None):
    scale = 1.0 / math.sqrt(hs)
    ctx = dq = None
    dkt, dvt = [], []
    if up is not None:
        upt = flip(up).astype(BF16)
        qt = flip(q).astype(BF16)
    for h in range(q.shape[1] // hs):
        s = dot_t(head_cols(h, hs, q), k) * scale
        if mask is not None:
            s = jnp.where(mask, s, -1e30)
        p = softmax(s)
        w = p.astype(BF16)
        if forward:
            c = dot(w, head_cols(h, hs, v))
            ctx = c if ctx is None else ctx + c
        if up is not None:
            dp = dot_t(head_cols(h, hs, up), v)
            dvt.append(dot(upt[h * hs : (h + 1) * hs], w))
            ds = (p * (dp - jnp.sum(dp * p, axis=-1, keepdims=True)) * scale).astype(BF16)
            d = dot(ds, head_cols(h, hs, k))
            dq = d if dq is None else dq + d
            dkt.append(dot(qt[h * hs : (h + 1) * hs], ds))
    out = []
    if forward:
        out.append(ctx.astype(BF16))
    if up is not None:
        out += [
            dq.astype(BF16),
            jnp.concatenate(dkt, 0).T.astype(BF16),
            jnp.concatenate(dvt, 0).T.astype(BF16),
        ]
    return out


def groups_of(ref):
    n = ref.shape[-1]
    return [slice(i, i + 128) for i in range(0, n, 128)]


def select_of(visible):
    n = visible.shape[1]
    lower = lax.broadcasted_iota(jnp.int32, (n, n), 0) <= lax.broadcasted_iota(jnp.int32, (n, n), 1)
    rank = dot(visible.astype(F32).astype(BF16), lower.astype(F32).astype(BF16))
    row = lax.broadcasted_iota(jnp.int32, (VP, n), 0).astype(F32) + 1.0
    picks = (row == rank) & (visible.astype(F32) > 0.5)
    return picks.astype(F32).astype(BF16)


def total(refs, index=None):
    acc = None
    for r in refs:
        x = (r[...] if index is None else r[index]).astype(F32)
        acc = x if acc is None else acc + x
    return acc


def seen_mask(rows):
    a = lax.broadcasted_iota(jnp.int32, (rows, rows), 0)
    b = lax.broadcasted_iota(jnp.int32, (rows, rows), 1)
    return (a // VP == b // VP) & (b % VP < VIS)


def seen_kernel(fut, vis, wenc, wemb, normed, proj, att, part):
    for j in range(fut.shape[0]):
        sel = select_of(vis[j : j + 1, :])
        seen = dot(sel, fut[j]).astype(BF16)
        normed[j * VP : (j + 1) * VP, :] = normalize(seen.astype(F32)).astype(BF16)
    x = normed[...]
    for c in range(3):
        proj[c] = dot(x, wenc[c]).astype(BF16)
    mask = seen_mask(x.shape[0])
    for g in groups_of(att):
        (att[:, g],) = attention(proj[0, :, g], proj[1, :, g], proj[2, :, g], HD, mask=mask)
    part[...] = dot(att[...], wemb[...]).astype(BF16)


def query_kernel(n_mp, vis, mask_token, pos, wq, wout, og, *refs):
    parts = refs[:n_mp]
    dec_in, normed, query, cgrad = refs[n_mp:]
    for j in range(og.shape[0]):
        v = vis[j : j + 1, :]
        sel = select_of(v)
        emb = total(parts, (slice(j * VP, (j + 1) * VP), slice(None))).astype(BF16)
        placed = dot(flip(sel).astype(BF16), emb)
        hidden = 1.0 - flip(jnp.broadcast_to(v, (8, v.shape[1])))[:, :1]
        d = (placed + hidden * mask_token[...].astype(F32) + pos[...].astype(F32)).astype(BF16)
        dec_in[j] = d
        x = normalize(d.astype(F32)).astype(BF16)
        normed[j] = x
        query[j] = dot(x, wq[0]).astype(BF16)
        cgrad[j] = dot_t(og[j], wout[...]).astype(BF16)


def encode_kernel(n_mp, where, *refs):
    parts = refs[:n_mp]
    wenc, wemb, normed, proj, att, part, whole = refs[n_mp:]
    span = parts[0].shape[1]
    for k in range(n_mp):
        whole[:, pl.ds(pl.multiple_of(where[k] * span, span), span)] = parts[k][...]
    normed[...] = normalize(whole[...].astype(F32)).astype(BF16)
    for c in range(3):
        proj[c] = dot(normed[...], wenc[c]).astype(BF16)
    for g in groups_of(att):
        (att[:, g],) = attention(proj[0, :, g], proj[1, :, g], proj[2, :, g], HD)
    part[...] = dot(att[...], wemb[...]).astype(BF16)


def decode_kernel(j, n_mp, vis, pos, wqkv, wout, query, cgrad, *refs):
    parts = refs[:n_mp]
    paired, ctx, dq, dk, dv, update, pair_part, vis_part, keys, values = refs[n_mp:]
    emb = total(parts).astype(BF16)
    paired[...] = (emb.astype(F32) + pos[...].astype(F32)).astype(BF16)
    keys[...] = dot(paired[...], wqkv[1]).astype(BF16)
    values[...] = dot(paired[...], wqkv[2]).astype(BF16)
    for g in groups_of(ctx):
        ctx[:, g], dq[:, g], dk[:, g], dv[:, g] = attention(
            query[j, :, g], keys[:, g], values[:, g], DHD, up=cgrad[j, :, g]
        )
    pair_part[...] = (dot_t(dk[...], wqkv[1]) + dot_t(dv[...], wqkv[2])).astype(BF16)
    chosen = dot(select_of(vis[j : j + 1, :]), dq[...]).astype(BF16)
    vis_part[...] = dot_t(chosen, wqkv[0]).astype(BF16)
    update[...] = dot(ctx[...], wout[...]).astype(BF16)


def decoder_weights_kernel(normed, og, p0, p1, c0, c1, q0, q1, k0, k1, v0, v1, qkv, wout):
    def term(a0, a1, b0, b1):
        return dot(flip(a0).astype(BF16), b0) + dot(flip(a1).astype(BF16), b1)

    qkv[0] = term(normed[0], normed[1], q0[...], q1[...]).astype(qkv.dtype)
    pt0, pt1 = flip(p0[...]).astype(BF16), flip(p1[...]).astype(BF16)
    qkv[1] = (dot(pt0, k0[...]) + dot(pt1, k1[...])).astype(qkv.dtype)
    qkv[2] = (dot(pt0, v0[...]) + dot(pt1, v1[...])).astype(qkv.dtype)
    wout[...] = term(c0[...], c1[...], og[0], og[1]).astype(wout.dtype)


def encode_back_kernel(n_mp, wemb, proj, *refs):
    parts = refs[:n_mp]
    grad, dproj, att_grad = refs[n_mp:]
    grad[...] = total(parts).astype(BF16)
    att_grad[...] = dot_t(grad[...], wemb[...]).astype(BF16)
    for g in groups_of(att_grad):
        dproj[0, :, g], dproj[1, :, g], dproj[2, :, g] = attention(
            proj[0, :, g], proj[1, :, g], proj[2, :, g], HD, up=att_grad[:, g], forward=False
        )


def seen_back_kernel(n_mp, vis, og, dec_in, wemb, proj, *refs):
    parts = (refs[:n_mp], refs[n_mp : 2 * n_mp])
    grad, dproj, att_grad = refs[2 * n_mp :]
    for j in range(2):
        sel = select_of(vis[j : j + 1, :])
        cot = total(parts[j])
        wide = dot(sel, dec_in[j])
        out = dot(sel, og[j])
        centred = wide - jnp.mean(wide, axis=-1, keepdims=True)
        inverse = lax.rsqrt(jnp.mean(centred * centred, axis=-1, keepdims=True) + EPS)
        unit = centred * inverse
        back = inverse * (
            cot
            - jnp.mean(cot, axis=-1, keepdims=True)
            - unit * jnp.mean(cot * unit, axis=-1, keepdims=True)
        )
        grad[j * VP : (j + 1) * VP, :] = (out + back).astype(BF16)
    att_grad[...] = dot_t(grad[...], wemb[...]).astype(BF16)
    mask = seen_mask(grad.shape[0])
    for g in groups_of(att_grad):
        dproj[0, :, g], dproj[1, :, g], dproj[2, :, g] = attention(
            proj[0, :, g], proj[1, :, g], proj[2, :, g], HD,
            up=att_grad[:, g], forward=False, mask=mask,
        )


def embed_weights_kernel(a0, a1, sa, g0, g1, sg, out):
    out[...] = (
        dot(flip(a0[...]).astype(BF16), g0[...])
        + dot(flip(a1[...]).astype(BF16), g1[...])
        + dot(flip(sa[...]).astype(BF16), sg[...])
    ).astype(out.dtype)


def encoder_weights_kernel(n0, n1, sn, d0, d1, sd, out):
    rows = 256
    for r in range(0, n0.shape[1], rows):
        cut = slice(r, r + rows)
        t0 = flip(n0[:, cut]).astype(BF16)
        t1 = flip(n1[:, cut]).astype(BF16)
        ts = flip(sn[:, cut]).astype(BF16)
        for c in range(3):
            out[c, cut, :] = (dot(t0, d0[c]) + dot(t1, d1[c]) + dot(ts, sd[c])).astype(out.dtype)


def tail_kernel(n_mp, n_groups, *refs):
    n = 3 + n_groups
    n_full = 3
    (qkv_own, out_own, wemb, proj0, proj1, att0, att1, seen_att, seen_grad, seen_dproj,
     n0, n1, sn) = refs[:13]
    refs = refs[13:]
    parts = (refs[:n_mp], refs[n_mp : 2 * n_mp])
    refs = refs[2 * n_mp :]
    outs = refs[:n]
    refs = refs[n:]
    emb_own, *enc_own = refs[: 1 + n_groups]
    refs = refs[1 + n_groups :]
    own = [qkv_own, out_own, emb_own, *enc_own]
    got_s, sum_s, got_a, sum_a, got_b = (refs[k * n : (k + 1) * n] for k in range(5))
    grads, att_grads, flipped, seen_flipped, send, recv = (
        refs[5 * n : 5 * n + 2], refs[5 * n + 2 : 5 * n + 4], refs[5 * n + 4 : 5 * n + 6],
        refs[5 * n + 6], refs[5 * n + 7], refs[5 * n + 8],
    )
    s = lax.axis_index("side")
    p = lax.axis_index("pair")
    hi, lo = p // 2, p % 2
    to_s = {"side": 1 - s}
    to_a = {"pair": hi * 2 + 1 - lo}
    to_b = {"pair": (1 - hi) * 2 + lo}

    barrier = pltpu.get_barrier_semaphore()
    for to in (to_s, to_a, to_b):
        pl.semaphore_signal(barrier, inc=1, device_id=to, device_id_type=pl.DeviceIdType.MESH)
    pl.semaphore_wait(barrier, 3)

    def start(i, stage, src, dst, to):
        copy = pltpu.make_async_remote_copy(
            src_ref=src, dst_ref=dst, send_sem=send.at[i, stage], recv_sem=recv.at[i, stage],
            device_id=to, device_id_type=pl.DeviceIdType.MESH,
        )
        copy.start()
        return copy

    def add(a, b):
        return a.astype(F32) + b.astype(F32)

    stage_s, stage_a, stage_b, gather = {}, {}, {}, {}

    def run_s(i):
        stage_s[i] = start(i, 0, own[i].at[:, :, 1 - s], got_s[i], to_s)

    def run_a(i):
        stage_s[i].wait()
        for h in range(2):
            for l in range(2):
                sum_s[i][h, l] = add(own[i][h, l, s], got_s[i][h, l]).astype(BF16)
        stage_a[i] = start(i, 1, sum_s[i].at[:, 1 - lo], got_a[i], to_a)

    def run_b(i):
        stage_a[i].wait()
        for h in range(2):
            sum_a[i][h] = add(sum_s[i][h, lo], got_a[i][h]).astype(BF16)
        stage_b[i] = start(i, 2, sum_a[i].at[1 - hi], got_b[i], to_b)

    def run_sum(i):
        stage_b[i].wait()
        block = add(sum_a[i][hi], got_b[i][...]).astype(outs[i].dtype)
        if i < n_full:
            outs[i][hi, lo, s] = block
            mine = outs[i].at[hi, lo, s]
            gather[i] = start(i, 3, mine, mine, to_b)
        else:
            outs[i][...] = block

    def run_g1(i):
        gather[i].wait()
        mine = outs[i].at[:, lo, s]
        gather[i] = start(i, 4, mine, mine, to_a)

    def run_g2(i):
        gather[i].wait()
        mine = outs[i].at[:, :, s]
        gather[i] = start(i, 5, mine, mine, to_s)

    def run_end(i):
        gather[i].wait()

    def blocks():
        return [(h, l, t) for h in range(2) for l in range(2) for t in range(2)]

    run_s(0)
    run_s(1)
    for j in range(2):
        grads[j][...] = total(parts[j]).astype(BF16)
    emb_rows = emb_own.shape[3]
    term = (
        dot(flip(att0[...]).astype(BF16), grads[0][...])
        + dot(flip(att1[...]).astype(BF16), grads[1][...])
        + dot(flip(seen_att[...]).astype(BF16), seen_grad[...])
    ).astype(BF16)
    for k, (h, l, t) in enumerate(blocks()):
        emb_own[h, l, t] = term[k * emb_rows : (k + 1) * emb_rows]
    run_s(2)
    run_a(0)
    run_a(1)
    for j in range(2):
        att_grads[j][...] = dot_t(grads[j][...], wemb[...]).astype(BF16)
    depth = n0.shape[1]
    step = depth // 4
    for r in range(0, depth, step):
        flipped[0][r : r + step, :] = flip(n0[:, r : r + step]).astype(BF16)
        flipped[1][r : r + step, :] = flip(n1[:, r : r + step]).astype(BF16)
        seen_flipped[r : r + step, :] = flip(sn[:, r : r + step]).astype(BF16)
    run_a(2)

    last = n_groups + 3
    later = {k: [] for k in range(last + 1)}

    def plan(f, i, at):
        later[min(at, last)].append(functools.partial(f, i))

    for g in range(n_groups):
        plan(run_a, n_full + g, g + 1)
    for g in range(n_groups):
        plan(run_b, n_full + g, g + 3)
    for i in range(n_full):
        wait = i // 2
        plan(run_b, i, wait)
        plan(run_sum, i, wait + 2)
        plan(run_g1, i, wait + n_groups)
        plan(run_g2, i, wait + n_groups + 1)
    for g in range(n_groups):
        plan(run_sum, n_full + g, max(g + 4, n_groups + 2))
    for i in range(n_full):
        plan(run_end, i, last)

    eighth = depth // 8
    for g in range(n_groups):
        cut = slice(g * 128, (g + 1) * 128)
        both = []
        for j, proj in enumerate((proj0, proj1)):
            d = attention(
                proj[0, :, cut], proj[1, :, cut], proj[2, :, cut], HD,
                up=att_grads[j][:, cut], forward=False,
            )
            both.append(jnp.concatenate(d, 1))
        seen_d = jnp.concatenate([seen_dproj[c, :, cut] for c in range(3)], 1)
        for k, (h, l, t) in enumerate(blocks()):
            rows = slice(k * eighth, (k + 1) * eighth)
            block = (
                dot(flipped[0][rows, :], both[0])
                + dot(flipped[1][rows, :], both[1])
                + dot(seen_flipped[rows, :], seen_d)
            ).astype(BF16)
            for c in range(3):
                enc_own[g][h, l, t, c * eighth : (c + 1) * eighth, :] = block[
                    :, c * 128 : (c + 1) * 128
                ]
        run_s(n_full + g)
        for f in later[g]:
            f()
    for k in range(n_groups, last + 1):
        for f in later[k]:
            f()


def tail(qkv_term, out_term, args, parts0, parts1):
    wemb, np_, depth, ew = args[0], args[1].shape[1], args[8].shape[1], args[1].shape[2]
    n_groups = ew // 128
    eight = (2, 2, 2)
    emb_tail = (wemb.shape[0] // 8, wemb.shape[1])
    enc_tail = (3 * depth // 8, 128)
    tails = [qkv_term.shape[3:], out_term.shape[3:], emb_tail] + [enc_tail] * n_groups
    outs = [(eight + t) for t in tails[:3]] + tails[3:]
    scratch = [pltpu.VMEM(eight + t, BF16) for t in tails[2:]]
    for lead in ((2, 2), (2, 2), (2,), (2,), ()):
        scratch += [pltpu.VMEM(lead + t, BF16) for t in tails]
    dd, sr = wemb.shape[1], args[7].shape[1]
    n = len(tails)
    scratch += [pltpu.VMEM((np_, dd), BF16)] * 2 + [pltpu.VMEM((np_, ew), BF16)] * 2
    scratch += [pltpu.VMEM((depth, np_), BF16)] * 2 + [pltpu.VMEM((depth, sr), BF16)]
    scratch += [pltpu.SemaphoreType.DMA((n, 6))] * 2
    operands = (qkv_term, out_term, *args, *parts0, *parts1)
    return pl.pallas_call(
        functools.partial(tail_kernel, len(parts0), n_groups),
        out_shape=[jax.ShapeDtypeStruct(sh, BF16) for sh in outs],
        in_specs=[pl.BlockSpec(memory_space=pltpu.VMEM)] * len(operands),
        out_specs=[pl.BlockSpec(memory_space=pltpu.VMEM)] * n,
        scratch_shapes=scratch,
        compiler_params=pltpu.CompilerParams(
            vmem_limit_bytes=VMEM_LIMIT, collective_id=0, has_side_effects=True
        ),
    )(*operands)


def widen_kernel(n_groups, *refs):
    ins, outs = refs[: 3 + n_groups], refs[3 + n_groups :]
    for a, b in zip(ins[:3], outs[:3]):
        b[...] = a[...].astype(F32)
    rows = outs[3].shape[1]
    for g, a in enumerate(ins[3:]):
        for c in range(3):
            outs[3][c, :, g * 128 : (g + 1) * 128] = a[c * rows : (c + 1) * rows, :].astype(F32)


def call(kernel, outs, args, scratch=(), smem=0, flops=0):
    specs = [pl.BlockSpec(memory_space=pltpu.SMEM)] * smem
    specs += [pl.BlockSpec(memory_space=pltpu.VMEM)] * (len(args) - smem)
    bytes_moved = sum(a.size * a.dtype.itemsize for a in args) + sum(
        math.prod(s) * jnp.dtype(t).itemsize for s, t in outs
    )
    return pl.pallas_call(
        kernel,
        out_shape=[jax.ShapeDtypeStruct(s, t) for s, t in outs],
        in_specs=specs,
        out_specs=[pl.BlockSpec(memory_space=pltpu.VMEM)] * len(outs),
        scratch_shapes=[pltpu.VMEM(s, t) for s, t in scratch],
        compiler_params=pltpu.CompilerParams(vmem_limit_bytes=VMEM_LIMIT),
        cost_estimate=pl.CostEstimate(
            flops=flops, bytes_accessed=bytes_moved, transcendentals=0
        ),
    )(*args)


def shifted(x, axis, k):
    n = lax.axis_size(axis)
    return lax.ppermute(x, axis, [(i, (i + k) % n) for i in range(n)])


def all_parts(x):
    return [x] + [shifted(x, "mp", k) for k in range(1, lax.axis_size("mp"))]


def body(past, future, visible, partner, wenc, wemb, mask_token, pos, wqkv, wout, og):
    frames, np_, width = past.shape
    dd = pos.shape[1]
    n_mp = lax.axis_size("mp")
    half = lax.axis_size("pair") // 2
    ew, dw = wenc.shape[2], wqkv.shape[2]
    big = 6_000_000_000

    me = lax.axis_index("mp")
    where = (me - jnp.arange(n_mp, dtype=jnp.int32)) % n_mp
    wanted = shifted(partner, "pair", half)[0]
    span = width // n_mp
    strip = lax.dynamic_slice_in_dim(past, me * span, span, axis=2)
    strips = [jnp.where(wanted[j] == 0, strip[0], strip[1]) for j in range(frames)]

    first, future = lax.optimization_barrier((strips[0], future))
    early = shifted(first, "pair", half)
    sr = frames * VP
    seen_normed, seen_proj, seen_att, seen_part = call(
        seen_kernel,
        [((sr, width), BF16), ((3, sr, ew), BF16), ((sr, ew), BF16), ((sr, dd), BF16)],
        (future, visible, wenc, wemb), flops=big // 4,
    )
    late, seen_part = lax.optimization_barrier((strips[1], seen_part))
    late = shifted(late, "pair", half)
    arrived = [all_parts(early), all_parts(late)]
    dec_in, normed_dec, query, cgrad = call(
        functools.partial(query_kernel, n_mp),
        [((frames, np_, dd), BF16)] * 2 + [((frames, np_, dw), BF16)] * 2,
        (visible, mask_token.reshape(1, dd), pos, wqkv, wout, og, *all_parts(seen_part)),
        flops=big // 4,
    )
    arrived[0][0], query = lax.optimization_barrier((arrived[0][0], query))
    enc = [
        call(
            functools.partial(encode_kernel, n_mp),
            [((np_, width), BF16), ((3, np_, ew), BF16), ((np_, ew), BF16), ((np_, dd), BF16)],
            (where, *arrived[j], wenc, wemb), smem=1, flops=big,
            scratch=[((np_, width), BF16)],
        )
        for j in range(frames)
    ]
    emb_parts = [all_parts(e[3]) for e in enc]
    dec = [
        call(
            functools.partial(decode_kernel, j, n_mp),
            [((np_, dd), BF16)] + [((np_, dw), BF16)] * 4
            + [((np_, dd), BF16)] * 2 + [((VP, dd), BF16)],
            (visible, pos, wqkv, wout, query, cgrad, *emb_parts[j]),
            scratch=[((np_, dw), BF16)] * 2, flops=big,
        )
        for j in range(frames)
    ]
    paired, ctx, dq, dk, dv, update, pair_part, vis_part = zip(*dec)
    pair_parts = [all_parts(x) for x in pair_part]
    vis_parts = [all_parts(x) for x in vis_part]
    updates = [all_parts(x) for x in update]
    qkv_term, out_term = call(
        decoder_weights_kernel,
        [(wqkv.shape, BF16), (wout.shape, BF16)],
        (normed_dec, og, *paired, *ctx, *dq, *dk, *dv), flops=big // 2,
    )
    seen_grad, seen_dproj = call(
        functools.partial(seen_back_kernel, n_mp),
        [((sr, dd), BF16), ((3, sr, ew), BF16)],
        (visible, og, dec_in, wemb, seen_proj, *vis_parts[0], *vis_parts[1]),
        scratch=[((sr, ew), BF16)], flops=big // 4,
    )
    prediction = jnp.stack([
        (dec_in[j].astype(F32) + sum(u.astype(F32) for u in updates[j])).astype(BF16)
        for j in range(frames)
    ])
    if lax.axis_size("pair") == 4:
        def split(x):
            return x.reshape(2, 2, 2, x.shape[0] // 8, x.shape[1])

        sums = tail(
            split(qkv_term.reshape(-1, dw)), split(out_term),
            (wemb, enc[0][1], enc[1][1], enc[0][2], enc[1][2], seen_att, seen_grad, seen_dproj,
             enc[0][0], enc[1][0], seen_normed),
            pair_parts[0], pair_parts[1],
        )
        shapes = [(3 * dd, dw), wout.shape, wemb.shape]
        dense = [x.reshape(sh) for x, sh in zip(sums[:3], shapes)]
        qkv_grad, out_grad, embed_grad, enc_grad = call(
            functools.partial(widen_kernel, ew // 128),
            [(x.shape, F32) for x in dense] + [((3, width // 8, ew), F32)],
            (*dense, *sums[3:]),
        )
        qkv_grad = qkv_grad.reshape(wqkv.shape)
    else:
        back = [
            call(
                functools.partial(encode_back_kernel, n_mp),
                [((np_, dd), BF16), ((3, np_, ew), BF16)],
                (wemb, enc[j][1], *pair_parts[j]),
                scratch=[((np_, ew), BF16)], flops=big,
            )
            for j in range(frames)
        ]
        (embed_term,) = call(
            embed_weights_kernel, [(wemb.shape, BF16)],
            (enc[0][2], enc[1][2], seen_att, back[0][0], back[1][0], seen_grad), flops=big // 4,
        )
        (enc_term,) = call(
            encoder_weights_kernel, [(wenc.shape, BF16)],
            (enc[0][0], enc[1][0], seen_normed, back[0][1], back[1][1], seen_dproj), flops=big,
        )
        enc_grad = lax.psum_scatter(
            enc_term, ("pair", "side"), scatter_dimension=1, tiled=True
        ).astype(F32)
        embed_grad, qkv_grad, out_grad = (
            x.astype(F32)
            for x in lax.psum((embed_term, qkv_term, out_term), ("pair", "side"))
        )
    return (prediction, enc_grad, embed_grad, qkv_grad, out_grad)


def solution(mesh):
    rows = ("groups", "pair", "side")
    in_specs = (
        P(rows, None, None),
        P(rows, None, None),
        P(rows, None),
        P(rows, None),
        P(None, None, "mp"),
        P("mp", None),
        P(),
        P(),
        P(None, None, "mp"),
        P("mp", None),
        P(rows, None, None),
    )
    out_specs = (
        P(rows, None, None),
        P("groups", ("pair", "side"), "mp"),
        P(("groups", "mp"), None),
        P("groups", None, "mp"),
        P(("groups", "mp"), None),
    )
    return jax.shard_map(body, mesh=mesh, in_specs=in_specs, out_specs=out_specs, check_vma=False)
```
